32 devices in a mesh: groups: 2 (over x), feat: 8 (over z, y), rep: 2 (over core).
Axes of the slice: x: 2, y: 2, z: 4, core: 2. Of those that a mesh axis runs over, the one named last changes fastest.
Arguments:
- seed_feat: bfloat16 [4, 768, 256], P(('groups', 'rep'), 'feat'), parts along dimension 0, may hold values from -6 to 6
- hop_feat: bfloat16 [4, 768, 8, 256], P(('groups', 'rep'), 'feat'), parts along dimension 0, may hold values from -6 to 6
- frontier: bfloat16 [4, 768, 6144], P(('groups', 'rep'), 'feat'), parts along dimension 0, may hold values from -6 to 6
- nbr_index: int32 [4, 4, 8, 256], P(('groups', 'rep')), parts along dimension 0, may hold values from 0 to 6143
- hop_degree: int32 [4, 8, 256], P(('groups', 'rep')), parts along dimension 0, may hold values from 1 to 4
- seed_degree: int32 [4, 256], P(('groups', 'rep')), parts along dimension 0, may hold values from 1 to 8
- w_self: bfloat16 [768, 512], P('feat'), may hold values from -0.21875 to 0.21875
- w_neigh: bfloat16 [768, 512], P('feat'), may hold values from -0.21875 to 0.21875
- v_self: bfloat16 [512, 153], replicated, may hold values from -0.25 to 0.25
- v_neigh: bfloat16 [512, 153], replicated, may hold values from -0.25 to 0.25
- cotangent: bfloat16 [4, 256, 153], P(('groups', 'rep'), 'feat'), parts along dimension 0, may hold values from -6 to 6
Outputs:
- logits: bfloat16 [4, 256, 153], P(('groups', 'rep'), 'feat'), parts along dimension 0
- grad_w_self: float32 [1536, 512], P(('groups', 'feat')), parts along dimension 0
- grad_w_neigh: float32 [1536, 512], P(('groups', 'feat')), parts along dimension 0
- grad_v_self: float32 [1024, 153], P('groups'), parts along dimension 0
- grad_v_neigh: float32 [1024, 153], P('groups'), parts along dimension 0
The draws below stay inside these ranges and needn't reach their ends.
There are 2 independent parts, one for each index of `groups`. The reference program is written for one: setup_inputs(seed, part) draws one part's arguments, and reference() takes and returns one part's arrays. A program takes and returns all parts, laid end to end along the dimension named above; an argument that names none is the same for every part. Nothing has to cross between parts.
Inputs may be any that keep to these rules, and one draw needn't show every extreme that they name: nbr_index names a column of its own half's frontier.
All inputs are finite; a program needn't handle non-finite values.
Results may differ from the reference program's by a relative error of at most 0.0075.
Values may be sent and summed in bfloat16 or wider, within the bound.
No kernel may reach another device: no remote copies, remote signals or barrier semaphores. Data moves between devices by JAX's collectives and lax.ppermute only.
A program may use at most 128 MiB of HBM per device.

```python
import jax
import jax.numpy as jnp

F = 768
C = 153
H = 512
FAN1 = 8
FAN2 = 4
HALF = 256
UNIQ = 6144
N_REP = 2


def place_ends(result, rng, smallest, largest):
    longest = result.shape.index(max(result.shape))
    spots = []
    for shift in (0, 1):
        where = [jax.random.randint(jax.random.fold_in(rng, axis), (), 0, length) for axis, length in enumerate(result.shape)]
        where[longest] = (where[longest] + shift) % result.shape[longest]
        spots.append(tuple(where))
    return result.at[spots[0]].set(smallest).at[spots[1]].set(largest)


def steps_of(rng, dims, cuts, low, high):
    level = 1.0
    for position, parts in cuts:
        draws = jax.random.uniform(jax.random.fold_in(jax.random.fold_in(rng, 6), position), (parts,), jnp.float32, low / len(cuts), high / len(cuts))
        level = level * jnp.repeat(jnp.exp(draws), dims[position] // parts).reshape((-1,) + (1,) * (len(dims) - 1 - position))
    return level


def noise(stream_key, shape, spread, reach, pieces=(), kind=jnp.bfloat16):
    values = jax.random.normal(stream_key, shape, jnp.float32) * spread
    if len(pieces) > 0:
        values = steps_of(stream_key, shape, pieces, -0.22, 0.18) * values
    return jnp.clip(values, min=-reach, max=reach).astype(kind)


def setup_inputs(seed: int = 0, part: int = 0) -> dict:
    arg_keys = jax.random.split(jax.random.key(seed), 12)
    own_keys = jax.random.split(jax.random.fold_in(arg_keys[11], part), 12)
    seed_feat = noise(own_keys[0], (N_REP, F, HALF), 1.0, 6.0, ((0, 2), (1, 8)))
    hop_feat = noise(own_keys[1], (N_REP, F, FAN1, HALF), 1.0, 6.0, ((0, 2), (1, 8)))
    frontier = noise(own_keys[2], (N_REP, F, UNIQ), 1.0, 6.0, ((0, 2), (1, 8)))
    nbr_index = place_ends(jax.random.randint(own_keys[3], (N_REP, FAN2, FAN1, HALF), 0, UNIQ), jax.random.fold_in(own_keys[3], 1), 0, UNIQ - 1).astype(jnp.int32)
    hop_degree = place_ends(jax.random.randint(own_keys[4], (N_REP, FAN1, HALF), 1, FAN2 + 1), jax.random.fold_in(own_keys[4], 1), 1, FAN2).astype(jnp.int32)
    seed_degree = place_ends(jax.random.randint(own_keys[5], (N_REP, HALF), 1, FAN1 + 1), jax.random.fold_in(own_keys[5], 1), 1, FAN1).astype(jnp.int32)
    w_self = noise(arg_keys[6], (F, H), F ** -0.5, 0.21875, ((0, 8),))
    w_neigh = noise(arg_keys[7], (F, H), F ** -0.5, 0.21875, ((0, 8),))
    v_self = noise(arg_keys[8], (H, C), H ** -0.5, 0.25)
    v_neigh = noise(arg_keys[9], (H, C), H ** -0.5, 0.25)
    cotangent = noise(own_keys[10], (N_REP, HALF, C), 1.0, 6.0, ((0, 2), (1, 8)))
    return {"seed_feat": seed_feat, "hop_feat": hop_feat, "frontier": frontier, "nbr_index": nbr_index, "hop_degree": hop_degree, "seed_degree": seed_degree, "w_self": w_self, "w_neigh": w_neigh, "v_self": v_self, "v_neigh": v_neigh, "cotangent": cotangent}


def neighbour_mean(table, nbr_index, hop_degree):
    total = jnp.zeros((table.shape[0],) + nbr_index.shape[1:], jnp.float32)
    for slot_index in range(nbr_index.shape[0]):
        picked = jnp.take(table, nbr_index[slot_index], axis=1).astype(jnp.float32)
        live_slot = (hop_degree > slot_index).astype(jnp.float32)
        total = total + picked * live_slot[None]
    return (total / hop_degree.astype(jnp.float32)[None]).astype(jnp.bfloat16)


def seed_average(hop_feat, seed_degree):
    fan_count = hop_feat.shape[1]
    live_slot = (jnp.arange(fan_count, dtype=jnp.int32)[:, None] < seed_degree[None, :]).astype(jnp.float32)
    total = jnp.sum(hop_feat.astype(jnp.float32) * live_slot[None], axis=1)
    return (total / seed_degree.astype(jnp.float32)[None]).astype(jnp.bfloat16)


def reference(seed_feat, hop_feat, frontier, nbr_index, hop_degree, seed_degree, w_self, w_neigh, v_self, v_neigh, cotangent):
    own_list = []
    agg_list = []
    for half_index in range(N_REP):
        hop_mean = neighbour_mean(frontier[half_index], nbr_index[half_index], hop_degree[half_index])
        seed_mean = seed_average(hop_feat[half_index], seed_degree[half_index])
        own_list.append(jnp.concatenate([seed_feat[half_index][:, None], hop_feat[half_index]], axis=1))
        agg_list.append(jnp.concatenate([seed_mean[:, None], hop_mean], axis=1))
    own_all = jnp.stack(own_list).astype(jnp.float32)
    agg_all = jnp.stack(agg_list).astype(jnp.float32)
    pre = jnp.einsum('rfkn,fh->rnkh', own_all, w_self.astype(jnp.float32)) + jnp.einsum('rfkn,fh->rnkh', agg_all, w_neigh.astype(jnp.float32))
    sigma = jax.nn.sigmoid(pre)
    hidden = (pre * sigma).astype(jnp.bfloat16)
    fan_count = hop_feat.shape[2]
    live_slot = (jnp.arange(fan_count, dtype=jnp.int32)[None, None, :] < seed_degree[:, :, None]).astype(jnp.float32)
    degree_f = seed_degree.astype(jnp.float32)
    hidden32 = hidden.astype(jnp.float32)
    hidden_mean = (jnp.sum(hidden32[:, :, 1:] * live_slot[..., None], axis=2) / degree_f[..., None]).astype(jnp.bfloat16)
    seed_hidden = hidden32[:, :, 0]
    mean32 = hidden_mean.astype(jnp.float32)
    vs32 = v_self.astype(jnp.float32)
    vn32 = v_neigh.astype(jnp.float32)
    cot32 = cotangent.astype(jnp.float32)
    logits = (jnp.einsum('rnh,hc->rnc', seed_hidden, vs32) + jnp.einsum('rnh,hc->rnc', mean32, vn32)).astype(jnp.bfloat16)
    grad_v_self = jnp.einsum('rnh,rnc->hc', seed_hidden, cot32)
    grad_v_neigh = jnp.einsum('rnh,rnc->hc', mean32, cot32)
    back_seed = jnp.einsum('rnc,hc->rnh', cot32, vs32)
    back_mean = jnp.einsum('rnc,hc->rnh', cot32, vn32)
    back_hops = back_mean[:, :, None, :] * live_slot[..., None] / degree_f[:, :, None, None]
    back = jnp.concatenate([back_seed[:, :, None, :], back_hops], axis=2)
    slope = sigma * (1.0 + pre * (1.0 - sigma))
    dpre = (back * slope).astype(jnp.bfloat16).astype(jnp.float32)
    grad_w_self = jnp.einsum('rfkn,rnkh->fh', own_all, dpre)
    grad_w_neigh = jnp.einsum('rfkn,rnkh->fh', agg_all, dpre)
    return (logits, grad_w_self, grad_w_neigh, grad_v_self, grad_v_neigh)
```

```python
import jax
import jax.numpy as jnp
from jax import lax
from jax.sharding import PartitionSpec as P

F32 = jnp.float32
BF16 = jnp.bfloat16


def neighbour_mean(table, nbr_index, hop_degree):
    total = jnp.zeros((table.shape[0],) + nbr_index.shape[1:], F32)
    for slot_index in range(nbr_index.shape[0]):
        picked = jnp.take(table, nbr_index[slot_index], axis=1).astype(F32)
        live_slot = (hop_degree > slot_index).astype(F32)
        total = total + picked * live_slot[None]
    return (total / hop_degree.astype(F32)[None]).astype(BF16)


def by_owner(hop, owners):
    f, t, s = hop.shape
    return hop.reshape(f, t, owners, s // owners).transpose(2, 0, 1, 3).reshape(owners, f, -1)


def on_device(
    seed_feat,
    hop_feat,
    frontier,
    nbr_index,
    hop_degree,
    seed_degree,
    w_self,
    w_neigh,
    v_self,
    v_neigh,
    cotangent,
):
    owners = lax.axis_size("feat")
    position = lax.axis_index("feat")
    half = lax.axis_index("rep")
    seeds = cotangent.shape[1]
    width = w_self.shape[1]
    fan = hop_feat.shape[2]
    own_hop = lax.all_to_all(by_owner(hop_feat[0], owners), "feat", 0, 0, tiled=True)
    seed_out = seed_feat[0].reshape(-1, owners, seeds).transpose(1, 0, 2)
    own_seed = lax.all_to_all(seed_out, "feat", 0, 0, tiled=True).reshape(-1, seeds)
    w_half = jnp.where(half == 0, w_self, w_neigh)
    w_half = lax.all_gather(w_half, "feat", axis=0, tiled=True)
    w_full = lax.all_gather(w_half, "rep", axis=0, tiled=False)
    hop_mean = neighbour_mean(frontier[0], nbr_index[0], hop_degree[0])
    agg_hop = lax.all_to_all(by_owner(hop_mean, owners), "feat", 0, 0, tiled=True)
    own_hop = own_hop.reshape(-1, fan * seeds)
    agg_hop = agg_hop.reshape(-1, fan * seeds)
    degree = lax.dynamic_slice_in_dim(seed_degree[0], position * seeds, seeds)
    degree_f = degree.astype(F32)
    live = (jnp.arange(fan, dtype=jnp.int32)[:, None] < degree[None, :]).astype(F32)
    seed_mean = (
        jnp.sum(own_hop.reshape(-1, fan, seeds).astype(F32) * live[None], axis=1) / degree_f[None]
    ).astype(BF16)
    own = jnp.concatenate([own_hop, own_seed], axis=1)
    agg = jnp.concatenate([agg_hop, seed_mean], axis=1)
    over_first = (((0,), (0,)), ((), ()))
    pre = lax.dot_general(own, w_full[0], over_first, preferred_element_type=F32)
    pre = pre + lax.dot_general(agg, w_full[1], over_first, preferred_element_type=F32)
    sigma = jax.nn.sigmoid(pre)
    hidden = (pre * sigma).astype(BF16)
    hops = fan * seeds
    seed_hidden = hidden[hops:]
    hidden_mean = (
        jnp.sum(hidden[:hops].reshape(fan, seeds, width).astype(F32) * live[:, :, None], axis=0)
        / degree_f[:, None]
    ).astype(BF16)
    logits = (
        jnp.dot(seed_hidden, v_self, preferred_element_type=F32)
        + jnp.dot(hidden_mean, v_neigh, preferred_element_type=F32)
    ).astype(BF16)
    cot = cotangent[0]
    over_classes = (((1,), (1,)), ((), ()))
    back_seed = lax.dot_general(cot, v_self, over_classes, preferred_element_type=F32)
    back_mean = lax.dot_general(cot, v_neigh, over_classes, preferred_element_type=F32)
    back_hops = back_mean[None] * live[:, :, None] / degree_f[None, :, None]
    back = jnp.concatenate([back_hops.reshape(hops, width), back_seed], axis=0)
    dpre = (back * sigma * (1.0 + pre * (1.0 - sigma))).astype(BF16)

    def swap(x):
        return lax.ppermute(x, "rep", [(0, 1), (1, 0)])

    mine = jnp.where(half == 0, own, agg)
    other = swap(jnp.where(half == 0, agg, own))
    dpre_other = swap(dpre)
    my_hidden = jnp.where(half == 0, seed_hidden, hidden_mean)
    other_hidden = swap(jnp.where(half == 0, hidden_mean, seed_hidden))
    partial = jnp.dot(mine, dpre, preferred_element_type=F32)
    partial = partial + jnp.dot(other, dpre_other, preferred_element_type=F32)
    blocks = lax.all_to_all(
        partial.astype(BF16).reshape(owners, -1, width), "feat", 0, 0, tiled=True
    )
    grad_w = jnp.sum(blocks.astype(F32), axis=0)
    hid = jnp.concatenate([my_hidden, other_hidden], axis=0)
    hid_all = lax.all_gather(hid, "feat", axis=0, tiled=False)
    cot_all = lax.all_gather(cot, "feat", axis=0, tiled=False)
    cot_other = swap(cot_all)
    cots = jnp.concatenate([cot_all, cot_other], axis=1)
    grad_v = lax.dot_general(
        hid_all, cots, (((0, 1), (0, 1)), ((), ())), preferred_element_type=F32
    )
    grad_w = lax.all_gather(grad_w, "rep", axis=0, tiled=False)
    grad_v = lax.all_gather(grad_v, "rep", axis=0, tiled=False)
    return (logits[None], grad_w[0], grad_w[1], grad_v[0], grad_v[1])


def solution(mesh):
    placed = (
        P(("groups", "rep"), "feat", None),
        P(("groups", "rep"), "feat", None, None),
        P(("groups", "rep"), "feat", None),
        P(("groups", "rep"), None, None, None),
        P(("groups", "rep"), None, None),
        P(("groups", "rep"), None),
        P("feat", None),
        P("feat", None),
        P(),
        P(),
        P(("groups", "rep"), "feat", None),
    )
    return jax.shard_map(
        on_device,
        mesh=mesh,
        in_specs=placed,
        out_specs=(
            P(("groups", "rep"), "feat", None),
            P(("groups", "feat"), None),
            P(("groups", "feat"), None),
            P("groups", None),
            P("groups", None),
        ),
        check_vma=False,
    )
```

```python
import functools

import jax
import jax.numpy as jnp
from jax import lax
from jax.experimental import pallas as pl
from jax.experimental.pallas import tpu as pltpu
from jax.sharding import PartitionSpec as P

F32 = jnp.float32
BF16 = jnp.bfloat16
LANES = 128
VMEM = pl.BlockSpec(memory_space=pltpu.VMEM)
SMEM = pl.BlockSpec(memory_space=pltpu.SMEM)
OVER_FIRST = (((0,), (0,)), ((), ()))
OVER_LAST = (((1,), (1,)), ((), ()))


def up(n, m):
    return -(-n // m) * m


def call(body, name, outs, in_specs, scratch=(), micros=1):
    return pl.pallas_call(
        body,
        name=name,
        out_shape=outs,
        in_specs=in_specs,
        out_specs=jax.tree.map(lambda _: VMEM, outs),
        scratch_shapes=list(scratch),
        compiler_params=pltpu.CompilerParams(vmem_limit_bytes=48 << 20),
        cost_estimate=pl.CostEstimate(
            flops=0, bytes_accessed=int(micros * 3_000_000), transcendentals=0
        ),
    )


def mix_groups(pieces, seeds, towards):
    groups = LANES // seeds
    shape = next(p for p in pieces if p is not None).shape
    lane_group = lax.broadcasted_iota(jnp.int32, shape, 1) // seeds
    total = jnp.zeros(shape, F32)
    for k, piece in enumerate(pieces):
        if piece is None:
            continue
        turn = (k - towards) % groups
        moved = pltpu.roll(piece, turn * seeds, axis=1) if turn else piece
        total = jnp.where(lane_group == k, moved, total)
    return total


def first_messages(sizes, half_ref, hop_ref, seed_ref, ws_ref, wn_ref, cot_ref, out_ref, hop32, seed32):
    owners, seeds, fan, f, fp, seed_rows, width, classes = sizes
    groups = LANES // seeds
    hops = fan * seeds
    parts = width // hops
    w_at = fp + seed_rows
    cot_at = w_at + parts * fp
    zeros = jnp.zeros((out_ref.shape[1], hops), BF16)

    if fp != f or classes != hops:
        for d in range(owners):
            out_ref[d] = zeros

    def put_weights(ref):
        for p in range(parts):
            block = ref[:, p * hops : (p + 1) * hops]
            for d in range(owners):
                out_ref[d, w_at + p * fp : w_at + p * fp + f, :] = block

    @pl.when(half_ref[0] == 0)
    def _():
        put_weights(ws_ref)

    @pl.when(half_ref[0] != 0)
    def _():
        put_weights(wn_ref)

    for d in range(owners):
        out_ref[d, cot_at : cot_at + seeds, :classes] = cot_ref[0]

    for tile in range(owners // groups):
        at = slice(tile * LANES, (tile + 1) * LANES)
        hop32[tile] = hop_ref[0, :, :, at].astype(F32).reshape(f * fan, LANES)
        for block in range(fan // groups):
            taken = [
                hop32[tile, pl.ds(block * groups + k, f, stride=fan), :] for k in range(groups)
            ]
            for e in range(groups):
                out_ref[tile * groups + e, :f, block * LANES : (block + 1) * LANES] = mix_groups(
                    taken, seeds, e
                ).astype(BF16)
    if fp != f:
        seed32[...] = jnp.zeros_like(seed32)
    seed32[:f, :] = seed_ref[0].astype(F32)
    bands = fp // 16
    for tile in range(owners // groups):
        at = slice(tile * LANES, (tile + 1) * LANES)
        for block in range(-(-bands // groups)):
            taken = [
                seed32[(block * groups + k) * 16 : (block * groups + k + 1) * 16, at]
                if block * groups + k < bands
                else None
                for k in range(groups)
            ]
            row, lane = divmod(block * LANES, hops)
            for e in range(groups):
                out_ref[
                    tile * groups + e, fp + row * 16 : fp + row * 16 + 16, lane : lane + LANES
                ] = mix_groups(taken, seeds, e).astype(BF16)


def gather_mean(sizes, idx_ref, deg_ref, table_ref, out_ref, rows, picked, live_idx, idx, sem):
    owners, seeds, fan, f, fp = sizes
    nodes = table_ref.shape[2]
    slots = idx_ref.shape[1]
    for u in range(slots):
        live_idx[u] = jnp.where(deg_ref[0] > u, idx_ref[0, u], nodes)
    load = pltpu.make_async_copy(live_idx, idx, sem)
    load.start()
    step = 512 if nodes % 512 == 0 else LANES
    lanes = rows.shape[1]
    tail = (lax.broadcasted_iota(jnp.int32, (lanes - f, step), 0) == 0).astype(F32)

    def flip(i, _):
        at = pl.multiple_of(i * step, step)
        block = jnp.concatenate([table_ref[0, :, pl.ds(at, step)].astype(F32), tail], axis=0)
        rows[pl.ds(at, step), :] = block.T
        return 0

    lax.fori_loop(0, nodes // step, flip, 0)
    rows[nodes:, :] = jnp.zeros((8, lanes), F32)
    load.wait()

    def owner_step(d, _):
        def slot_step(t, _):
            src = d * seeds
            for k in range(seeds):
                total = rows[pl.ds(idx[0, t, src + k], 1), :]
                for u in range(1, slots):
                    total = total + rows[pl.ds(idx[u, t, src + k], 1), :]
                picked[pl.ds(t * seeds + k, 1), :] = total
            return 0

        lax.fori_loop(0, fan, slot_step, 0)
        flat = picked[...].T
        mean = flat[:f] / flat[f : f + 1]
        if fp != f:
            mean = jnp.concatenate([mean, jnp.zeros((fp - f, mean.shape[1]), F32)], axis=0)
        out_ref[d] = mean.astype(BF16)
        return 0

    lax.fori_loop(0, owners, owner_step, 0)


def my_degrees(where_ref, seed_degree_ref, seeds):
    half = seed_degree_ref.shape[1]
    wide = jnp.broadcast_to(seed_degree_ref[...], (8, half))
    shift = lax.rem(half - where_ref[1] * seeds, half)
    mine = pltpu.roll(wide, shift, axis=1)[:, :LANES]
    lane = lax.broadcasted_iota(jnp.int32, (8, LANES), 1)
    return jnp.where(lane < seeds, mine, 1)


def stack_features(sizes, where_ref, seed_degree_ref, first_ref, agg_ref, own_ref, mean_ref, send_ref):
    owners, seeds, fan, fp, seed_rows = sizes
    groups = LANES // seeds
    hops = fan * seeds
    depth = owners * fp
    own = first_ref[:, :fp, :].reshape(depth, hops)
    own_ref[:, :hops] = own
    mean_ref[:, :hops] = agg_ref[...].reshape(depth, hops)
    lane = lax.broadcasted_iota(jnp.int32, (16, LANES), 1)
    for c in range(owners):
        for band in range(fp // 16):
            row, place = divmod(band * seeds, hops)
            tile = place // LANES
            block = first_ref[
                c, fp + row * 16 : fp + row * 16 + 16, tile * LANES : (tile + 1) * LANES
            ].astype(F32)
            turn = (-(band % groups)) % groups
            if turn:
                block = pltpu.roll(block, turn * seeds, axis=1)
            at = c * fp + band * 16
            own_ref[at : at + 16, hops:] = jnp.where(lane < seeds, block, 0.0).astype(BF16)
    degree = my_degrees(where_ref, seed_degree_ref, seeds)[:1]
    node = lax.broadcasted_iota(jnp.int32, (hops, LANES), 0)
    seed = lax.broadcasted_iota(jnp.int32, (hops, LANES), 1)
    live = (node % seeds == seed) & (node // seeds < degree)
    total = jnp.dot(own, live.astype(F32).astype(BF16), preferred_element_type=F32)
    mean_ref[:, hops:] = (total / degree.astype(F32)).astype(BF16)

    @pl.when(where_ref[0] == 0)
    def _():
        send_ref[...] = mean_ref[...]

    @pl.when(where_ref[0] != 0)
    def _():
        send_ref[...] = own_ref[...]


def forward(
    sizes,
    where_ref,
    seed_degree_ref,
    own_ref,
    mean_ref,
    w_mine_ref,
    w_other_ref,
    vs_ref,
    vn_ref,
    cot_ref,
    logits_ref,
    hidden_ref,
    dpre_ref,
    ws,
    wn,
):
    owners, seeds, fan, fp, w_at, width = sizes
    hops = fan * seeds
    depth = owners * fp
    parts = width // hops

    def lay(w_mine, w_other):
        for p in range(parts):
            at = slice(p * hops, (p + 1) * hops)
            rows = slice(w_at + p * fp, w_at + (p + 1) * fp)
            w_mine[:, at] = w_mine_ref[:, rows, :].reshape(depth, hops)
            w_other[:, at] = w_other_ref[:, p * fp : (p + 1) * fp, :].reshape(depth, hops)

    @pl.when(where_ref[0] == 0)
    def _():
        lay(ws, wn)

    @pl.when(where_ref[0] != 0)
    def _():
        lay(wn, ws)

    pre = lax.dot_general(own_ref[...], ws[...], OVER_FIRST, preferred_element_type=F32)
    pre = pre + lax.dot_general(mean_ref[...], wn[...], OVER_FIRST, preferred_element_type=F32)
    pre = pre[: hops + seeds]
    sigma = jax.nn.sigmoid(pre)
    hidden = (pre * sigma).astype(BF16)
    slope = sigma * (1.0 + pre * (1.0 - sigma))
    degree = my_degrees(where_ref, seed_degree_ref, seeds).astype(F32)
    degree = jnp.broadcast_to(degree[:1], (LANES, LANES)).T[:seeds]
    degree = jnp.concatenate([degree] * (width // LANES), axis=1)
    total = jnp.zeros((seeds, width), F32)
    for t in range(fan):
        row = hidden[t * seeds : (t + 1) * seeds].astype(F32)
        total = total + jnp.where(degree > t, row, 0.0)
    hidden_mean = (total / degree).astype(BF16)
    seed_hidden = hidden[hops:]
    hidden_ref[0] = seed_hidden
    hidden_ref[1] = hidden_mean
    logits = jnp.dot(seed_hidden, vs_ref[...], preferred_element_type=F32)
    logits = logits + jnp.dot(hidden_mean, vn_ref[...], preferred_element_type=F32)
    logits_ref[0] = logits.astype(BF16)
    cot = cot_ref[0]
    back_seed = lax.dot_general(cot, vs_ref[...], OVER_LAST, preferred_element_type=F32)
    back_mean = lax.dot_general(cot, vn_ref[...], OVER_LAST, preferred_element_type=F32)
    back_mean = back_mean / degree
    for t in range(fan):
        at = slice(t * seeds, (t + 1) * seeds)
        dpre_ref[at, :] = (jnp.where(degree > t, back_mean, 0.0) * slope[at]).astype(BF16)
    dpre_ref[hops : hops + seeds, :] = (back_seed * slope[hops:]).astype(BF16)
    dpre_ref[hops + seeds :, :] = jnp.zeros((LANES - seeds, width), BF16)


def second_messages(
    sizes, where_ref, own_ref, mean_ref, x_ref, dpre_ref, dpre_other_ref, hid_ref, hid_other_ref, out_ref
):
    owners, seeds, fp, width = sizes

    def products(mine_ref):
        total = jnp.dot(mine_ref[...], dpre_ref[...], preferred_element_type=F32)
        total = total + jnp.dot(x_ref[...], dpre_other_ref[...], preferred_element_type=F32)
        out_ref[:, :fp, :] = total.astype(BF16).reshape(owners, fp, width)

    @pl.when(where_ref[0] == 0)
    def _():
        products(own_ref)
        for d in range(owners):
            out_ref[d, fp : fp + seeds, :] = hid_ref[0]
            out_ref[d, fp + seeds :, :] = hid_other_ref[0]

    @pl.when(where_ref[0] != 0)
    def _():
        products(mean_ref)
        for d in range(owners):
            out_ref[d, fp : fp + seeds, :] = hid_ref[1]
            out_ref[d, fp + seeds :, :] = hid_other_ref[1]


def total_gradients(sizes, second_ref, cot_ref, cot_other_ref, grad_w_ref, grad_v_ref):
    owners, seeds, f, fp, width, cot_at = sizes
    total = second_ref[0, :fp, :].astype(F32)
    for c in range(1, owners):
        total = total + second_ref[c, :fp, :].astype(F32)
    grad_w_ref[...] = total[:f]
    hops = cot_ref.shape[2]
    flat = owners * seeds
    hid = second_ref[:, fp : fp + seeds, :].reshape(flat, width)
    hid_other = second_ref[:, fp + seeds : fp + 2 * seeds, :].reshape(flat, width)
    cot = cot_ref[:, cot_at : cot_at + seeds, :].reshape(flat, hops)
    cot_other = cot_other_ref[...].reshape(flat, hops)
    grad_v = lax.dot_general(hid, cot, OVER_FIRST, preferred_element_type=F32)
    grad_v = grad_v + lax.dot_general(hid_other, cot_other, OVER_FIRST, preferred_element_type=F32)
    grad_v_ref[...] = grad_v[:, : grad_v_ref.shape[1]]


def place_gradients(where_ref, w_mine, w_other, v_mine, v_other, ws_ref, wn_ref, vs_ref, vn_ref):
    @pl.when(where_ref[0] == 0)
    def _():
        ws_ref[...] = w_mine[...]
        wn_ref[...] = w_other[...]
        vs_ref[...] = v_mine[...]
        vn_ref[...] = v_other[...]

    @pl.when(where_ref[0] != 0)
    def _():
        ws_ref[...] = w_other[...]
        wn_ref[...] = w_mine[...]
        vs_ref[...] = v_other[...]
        vn_ref[...] = v_mine[...]


def swap(x):
    return lax.ppermute(x, "rep", [(0, 1), (1, 0)])


def spread(x):
    return lax.all_to_all(x, "feat", 0, 0, tiled=True)


def on_device(
    seed_feat,
    hop_feat,
    frontier,
    nbr_index,
    hop_degree,
    seed_degree,
    w_self,
    w_neigh,
    v_self,
    v_neigh,
    cotangent,
):
    owners = lax.axis_size("feat")
    where = jnp.stack([lax.axis_index("rep"), lax.axis_index("feat")]).astype(jnp.int32)
    seeds, classes = cotangent.shape[1:]
    f, width = w_self.shape
    fan = hop_feat.shape[2]
    nodes = frontier.shape[2]
    hops = fan * seeds
    fp = up(f, 16)
    seed_rows = 16 * -(-(fp // 16) * seeds // hops)
    w_rows = width // hops * fp
    w_at = fp + seed_rows
    cot_at = w_at + w_rows
    depth = owners * fp
    struct = jax.ShapeDtypeStruct

    first = call(
        functools.partial(
            first_messages, (owners, seeds, fan, f, fp, seed_rows, width, classes)
        ),
        "first_messages",
        struct((owners, cot_at + seeds, hops), BF16),
        [SMEM] + [VMEM] * 5,
        [
            pltpu.VMEM((owners * seeds // LANES, f * fan, LANES), F32),
            pltpu.VMEM((fp, owners * seeds), F32),
        ],
        micros=2,
    )(where, hop_feat, seed_feat, w_self, w_neigh, cotangent)
    first = spread(first)

    lanes = up(f + 1, LANES)
    agg = call(
        functools.partial(gather_mean, (owners, seeds, fan, f, fp)),
        "gather_mean",
        struct((owners, fp, hops), BF16),
        [VMEM] * 3,
        [
            pltpu.VMEM((nodes + 8, lanes), F32),
            pltpu.VMEM((hops, lanes), F32),
            pltpu.VMEM(nbr_index.shape[1:], jnp.int32),
            pltpu.SMEM(nbr_index.shape[1:], jnp.int32),
            pltpu.SemaphoreType.DMA,
        ],
        micros=14,
    )(nbr_index, hop_degree, frontier)
    agg = spread(agg)

    w_other = swap(first[:, w_at:cot_at])
    cot_other = swap(first[:, cot_at:])
    stacked = struct((depth, hops + LANES), BF16)
    own, mean, send = call(
        functools.partial(stack_features, (owners, seeds, fan, fp, seed_rows)),
        "stack_features",
        (stacked, stacked, stacked),
        [SMEM] + [VMEM] * 3,
    )(where, seed_degree, first, agg)
    x_other = swap(send)
    logits, hidden, dpre = call(
        functools.partial(forward, (owners, seeds, fan, fp, w_at, width)),
        "forward",
        (
            struct((1, seeds, classes), BF16),
            struct((2, seeds, width), BF16),
            struct((hops + LANES, width), BF16),
        ),
        [SMEM] + [VMEM] * 8,
        [pltpu.VMEM((depth, width), BF16), pltpu.VMEM((depth, width), BF16)],
        micros=5,
    )(where, seed_degree, own, mean, first, w_other, v_self, v_neigh, cotangent)
    second = call(
        functools.partial(second_messages, (owners, seeds, fp, width)),
        "second_messages",
        struct((owners, fp + 2 * seeds, width), BF16),
        [SMEM] + [VMEM] * 7,
        micros=3,
    )(where, own, mean, x_other, dpre, swap(dpre), hidden, swap(hidden))
    second = spread(second)
    grad_w, grad_v = call(
        functools.partial(total_gradients, (owners, seeds, f, fp, width, cot_at)),
        "total_gradients",
        (struct((f, width), F32), struct((width, classes), F32)),
        [VMEM] * 3,
    )(second, first, cot_other)
    grads = call(
        place_gradients,
        "place_gradients",
        (struct((f, width), F32),) * 2 + (struct((width, classes), F32),) * 2,
        [SMEM] + [VMEM] * 4,
    )(where, grad_w, swap(grad_w), grad_v, swap(grad_v))
    return (logits, *grads)


def solution(mesh):
    placed = (
        P(("groups", "rep"), "feat", None),
        P(("groups", "rep"), "feat", None, None),
        P(("groups", "rep"), "feat", None),
        P(("groups", "rep"), None, None, None),
        P(("groups", "rep"), None, None),
        P(("groups", "rep"), None),
        P("feat", None),
        P("feat", None),
        P(),
        P(),
        P(("groups", "rep"), "feat", None),
    )
    return jax.shard_map(
        on_device,
        mesh=mesh,
        in_specs=placed,
        out_specs=(
            P(("groups", "rep"), "feat", None),
            P(("groups", "feat"), None),
            P(("groups", "feat"), None),
            P("groups", None),
            P("groups", None),
        ),
        check_vma=False,
    )
```

```python
import functools

import jax
import jax.numpy as jnp
from jax import lax
from jax.experimental import pallas as pl
from jax.experimental.pallas import tpu as pltpu
from jax.sharding import PartitionSpec as P

F32 = jnp.float32
BF16 = jnp.bfloat16
LANES = 128
MICROS = 1
VMEM = pl.BlockSpec(memory_space=pltpu.VMEM)
SMEM = pl.BlockSpec(memory_space=pltpu.SMEM)
HBM = pl.BlockSpec(memory_space=pltpu.HBM)
OVER_FIRST = (((0,), (0,)), ((), ()))
OVER_LAST = (((1,), (1,)), ((), ()))


def up(n, m):
    return -(-n // m) * m


def call(body, name, outs, in_specs, scratch=(), micros=1, vmem=40):
    return pl.pallas_call(
        body,
        name=name,
        out_shape=outs,
        in_specs=in_specs,
        out_specs=jax.tree.map(lambda _: VMEM, outs),
        scratch_shapes=list(scratch),
        compiler_params=pltpu.CompilerParams(vmem_limit_bytes=vmem << 20),
        cost_estimate=pl.CostEstimate(
            flops=0, bytes_accessed=int(micros * 3_000_000), transcendentals=0
        ),
    )


def mix_groups(pieces, seeds, towards):
    groups = LANES // seeds
    shape = next(p for p in pieces if p is not None).shape
    lane_group = lax.broadcasted_iota(jnp.int32, shape, 1) // seeds
    total = jnp.zeros(shape, F32)
    for k, piece in enumerate(pieces):
        if piece is None:
            continue
        turn = (k - towards) % groups
        moved = pltpu.roll(piece, turn * seeds, axis=1) if turn else piece
        total = jnp.where(lane_group == k, moved, total)
    return total


def weight_message(sizes, ws_ref, wn_ref, cot_ref, out_ref, cot, sems):
    seeds, f, fp, classes = sizes
    width = out_ref.shape[1]
    split = seeds // 16

    def fetch(ref):
        loads = (
            pltpu.make_async_copy(ref, out_ref.at[pl.ds(0, f), :], sems.at[0]),
            pltpu.make_async_copy(cot_ref, cot, sems.at[1]),
        )
        for load in loads:
            load.start()
        for load in loads:
            load.wait()

    @pl.when(lax.axis_index("rep") == 0)
    def _():
        fetch(ws_ref)

    @pl.when(lax.axis_index("rep") != 0)
    def _():
        fetch(wn_ref)

    if fp != f:
        out_ref[f:fp, :] = jnp.zeros((fp - f, width), BF16)
    out_ref[fp:, :] = jnp.zeros((16, width), BF16)
    for p in range(split):
        at = p * (width // split)
        out_ref[fp:, at : at + classes] = cot[0, p * 16 : (p + 1) * 16, :]


def pack_features(
    sizes,
    idx_ref,
    deg_ref,
    table_ref,
    hop_ref,
    seed_ref,
    keep_ref,
    pass_ref,
    rows,
    live_ref,
    table,
    hop,
    packed,
    hop32,
    seed,
    seed32,
    deg,
    idx,
    sems,
):
    owners, seeds, fan, f, fp = sizes
    groups = LANES // seeds
    hops = fan * seeds
    nodes = table.shape[2]
    loads = [
        pltpu.make_async_copy(source, target, sems.at[i])
        for i, (source, target) in enumerate(
            ((idx_ref, idx), (deg_ref, deg), (hop_ref, hop), (seed_ref, seed), (table_ref, table))
        )
    ]
    for load in loads:
        load.start()
    for load in loads[:4]:
        load.wait()
    for u in range(idx.shape[1]):
        live_ref[u] = jnp.where(deg[0] > u, idx[0, u], nodes)
    if fp != f:
        packed[...] = jnp.zeros_like(packed)
        seed32[...] = jnp.zeros_like(seed32)
    for tile in range(owners // groups):
        at = slice(tile * LANES, (tile + 1) * LANES)
        hop32[tile] = hop[0, :, :, at].astype(F32).reshape(f * fan, LANES)
        for block in range(fan // groups):
            taken = [
                hop32[tile, pl.ds(block * groups + k, f, stride=fan), :] for k in range(groups)
            ]
            for e in range(groups):
                packed[tile * groups + e, :f, block * LANES : (block + 1) * LANES] = mix_groups(
                    taken, seeds, e
                ).astype(BF16)
    seed32[:f, :] = seed[0].astype(F32)
    bands = fp // 16
    for tile in range(owners // groups):
        at = slice(tile * LANES, (tile + 1) * LANES)
        for block in range(-(-bands // groups)):
            taken = [
                seed32[(block * groups + k) * 16 : (block * groups + k + 1) * 16, at]
                if block * groups + k < bands
                else None
                for k in range(groups)
            ]
            row, lane = divmod(block * LANES, hops)
            for e in range(groups):
                packed[
                    tile * groups + e, fp + row * 16 : fp + row * 16 + 16, lane : lane + LANES
                ] = mix_groups(taken, seeds, e).astype(BF16)

    side = lax.rem(lax.axis_index("feat"), 2)
    for j in range(owners // 2):
        keep_ref[j] = packed[2 * j + side]
        pass_ref[j] = packed[2 * j + 1 - side]

    loads[4].wait()
    step = 512 if nodes % 512 == 0 else LANES
    lanes = rows.shape[1]
    tail = (lax.broadcasted_iota(jnp.int32, (lanes - f, step), 0) == 0).astype(F32)

    def flip(i, _):
        at = pl.multiple_of(i * step, step)
        block = jnp.concatenate([table[0, :, pl.ds(at, step)].astype(F32), tail], axis=0)
        rows[pl.ds(at, step), :] = block.T
        return 0

    lax.fori_loop(0, nodes // step, flip, 0)
    rows[nodes:, :] = jnp.zeros((8, lanes), F32)


def gather_means(sizes, across_pair, begin, idx, rows, *rest):
    owners, seeds, fan, f, fp = sizes
    if len(rest) > 2:
        first, second, out_ref, joined, picked = rest
        joined[: first.shape[0], :] = first[...]
        joined[first.shape[0] :, :] = second[...]
    else:
        out_ref, picked = rest
    slots = idx.shape[0]
    hops = out_ref.shape[2]
    side = lax.rem(lax.axis_index("feat"), 2)
    if across_pair:
        side = 1 - side
    for j in range(out_ref.shape[0]):
        src = (2 * (begin + j) + side) * seeds

        def slot_step(t, _):
            for k in range(seeds):
                total = rows[pl.ds(idx[0, t, src + k], 1), :]
                for u in range(1, slots):
                    total = total + rows[pl.ds(idx[u, t, src + k], 1), :]
                picked[pl.ds(t * seeds + k, 1), :] = total
            return 0

        lax.fori_loop(0, fan, slot_step, 0)
        flat = picked[...].T
        mean = flat[:f] / flat[f : f + 1]
        if fp != f:
            mean = jnp.concatenate([mean, jnp.zeros((fp - f, hops), F32)], axis=0)
        out_ref[j] = mean.astype(BF16)


def merge_by_part(keeps, passes, outs):
    count, rows = len(outs), keeps[0].shape[1]
    each = count // len(keeps)
    me = lax.axis_index("feat") // 2
    for step, out_ref in enumerate(outs):
        owner = lax.rem(me + step, count)
        for part, (keep_ref, passed_ref) in enumerate(zip(keeps, passes)):

            @pl.when(owner // each == part)
            def _():
                out_ref[:rows, :] = keep_ref[owner - part * each]
                out_ref[rows:, :] = passed_ref[owner - part * each]


def merge_pairs(parts, *rest):
    keeps, passes, outs = rest[:parts], rest[parts : 2 * parts], rest[2 * parts :]
    count, rows = len(outs), keeps[0].shape[1]
    if parts > 1:
        merge_by_part(keeps, passes, outs)
        return
    keep_ref, passed_ref = keeps[0], passes[0]
    me = lax.axis_index("feat") // 2
    for step, out_ref in enumerate(outs):
        owner = lax.rem(me + step, count)
        out_ref[:rows, :] = keep_ref[owner]
        out_ref[rows:, :] = passed_ref[owner]


def my_degrees(seed_degree_ref, seeds):
    half = seed_degree_ref.shape[1]
    wide = jnp.broadcast_to(seed_degree_ref[...], (8, half))
    shift = lax.rem(half - lax.axis_index("feat") * seeds, half)
    mine = pltpu.roll(wide, shift, axis=1)[:, :LANES]
    lane = lax.broadcasted_iota(jnp.int32, (8, LANES), 1)
    return jnp.where(lane < seeds, mine, 1)


def stack_features(sizes, seed_degree_ref, *rest):
    owners, seeds, fan, fp, seed_rows = sizes
    half = owners // 2
    own_blocks, agg_blocks = rest[:half], rest[half:owners]
    own_ref, mean_ref, send_ref = rest[owners:]
    groups = LANES // seeds
    hops = fan * seeds
    own_rows = fp + seed_rows
    lane = lax.broadcasted_iota(jnp.int32, (16, LANES), 1)
    for c in range(owners):
        ref, low = own_blocks[c // 2], c % 2 * own_rows
        own_ref[c * fp : (c + 1) * fp, :hops] = ref[low : low + fp, :]
        mean_ref[c * fp : (c + 1) * fp, :hops] = agg_blocks[c // 2][c % 2 * fp : (c % 2 + 1) * fp, :]
        for band in range(fp // 16):
            row, place = divmod(band * seeds, hops)
            tile = place // LANES
            row = low + fp + row * 16
            block = ref[row : row + 16, tile * LANES : (tile + 1) * LANES].astype(F32)
            turn = (-(band % groups)) % groups
            if turn:
                block = pltpu.roll(block, turn * seeds, axis=1)
            at = c * fp + band * 16
            own_ref[at : at + 16, hops:] = jnp.where(lane < seeds, block, 0.0).astype(BF16)
    degree = my_degrees(seed_degree_ref, seeds)[:1]
    node = lax.broadcasted_iota(jnp.int32, (hops, LANES), 0)
    seed = lax.broadcasted_iota(jnp.int32, (hops, LANES), 1)
    live = (node % seeds == seed) & (node // seeds < degree)
    total = jnp.dot(own_ref[:, :hops], live.astype(F32).astype(BF16), preferred_element_type=F32)
    mean_ref[:, hops:] = (total / degree.astype(F32)).astype(BF16)

    @pl.when(lax.axis_index("rep") == 0)
    def _():
        send_ref[...] = mean_ref[...]

    @pl.when(lax.axis_index("rep") != 0)
    def _():
        send_ref[...] = own_ref[...]


def forward(
    sizes,
    seed_degree_ref,
    own_ref,
    mean_ref,
    near_ref,
    far_ref,
    near_other_ref,
    far_other_ref,
    vs_ref,
    vn_ref,
    cot_ref,
    logits_ref,
    hidden_ref,
    dpre_ref,
    ws,
    wn,
):
    owners, seeds, fan, fp, width, offsets = sizes
    hops = fan * seeds
    half = owners // 2
    me = lax.axis_index("feat")
    block = near_ref.shape[0] // half

    def lay(near, far, w):
        for p, offset in enumerate(offsets):
            source = jnp.bitwise_xor(me, offset)
            c = 2 * lax.rem(me // 2 + half - source // 2, half) + offset % 2
            ref, q = (near, p) if p < half else (far, p - half)
            to = pl.ds(pl.multiple_of(c * fp, fp), fp)
            w[to, :] = ref[q * block : q * block + fp, :]

    @pl.when(lax.axis_index("rep") == 0)
    def _():
        lay(near_ref, far_ref, ws)
        lay(near_other_ref, far_other_ref, wn)

    @pl.when(lax.axis_index("rep") != 0)
    def _():
        lay(near_ref, far_ref, wn)
        lay(near_other_ref, far_other_ref, ws)

    pre = lax.dot_general(own_ref[...], ws[...], OVER_FIRST, preferred_element_type=F32)
    pre = pre + lax.dot_general(mean_ref[...], wn[...], OVER_FIRST, preferred_element_type=F32)
    pre = pre[: hops + seeds]
    sigma = jax.nn.sigmoid(pre)
    hidden = (pre * sigma).astype(BF16)
    slope = sigma * (1.0 + pre * (1.0 - sigma))
    degree = my_degrees(seed_degree_ref, seeds).astype(F32)
    degree = jnp.broadcast_to(degree[:1], (LANES, LANES)).T[:seeds]
    degree = jnp.concatenate([degree] * (width // LANES), axis=1)
    total = jnp.zeros((seeds, width), F32)
    for t in range(fan):
        row = hidden[t * seeds : (t + 1) * seeds].astype(F32)
        total = total + jnp.where(degree > t, row, 0.0)
    hidden_mean = (total / degree).astype(BF16)
    seed_hidden = hidden[hops:]
    hidden_ref[0] = seed_hidden
    hidden_ref[1] = hidden_mean
    logits = lax.dot_general(seed_hidden, vs_ref[...], OVER_LAST, preferred_element_type=F32)
    logits = logits + lax.dot_general(
        hidden_mean, vn_ref[...], OVER_LAST, preferred_element_type=F32
    )
    logits_ref[0] = logits.astype(BF16)
    cot = cot_ref[0]
    back_seed = jnp.dot(cot, vs_ref[...], preferred_element_type=F32)
    back_mean = jnp.dot(cot, vn_ref[...], preferred_element_type=F32)
    back_mean = back_mean / degree
    for t in range(fan):
        at = slice(t * seeds, (t + 1) * seeds)
        dpre_ref[at, :] = (jnp.where(degree > t, back_mean, 0.0) * slope[at]).astype(BF16)
    dpre_ref[hops : hops + seeds, :] = (back_seed * slope[hops:]).astype(BF16)
    dpre_ref[hops + seeds :, :] = jnp.zeros((LANES - seeds, width), BF16)


def products(
    sizes,
    own_ref,
    mean_ref,
    x_ref,
    dpre_ref,
    dpre_other_ref,
    hid_ref,
    hid_other_ref,
    keep_ref,
    pass_ref,
    both_ref,
):
    owners, seeds, fp = sizes

    def run(mine_ref, part):
        total = jnp.dot(mine_ref[...], dpre_ref[...], preferred_element_type=F32)
        total = total + jnp.dot(x_ref[...], dpre_other_ref[...], preferred_element_type=F32)
        for c in range(owners):
            block = total[c * fp : (c + 1) * fp]
            if c % 2:
                pass_ref[c // 2] = block.astype(BF16)
            else:
                keep_ref[c // 2] = block
        both_ref[:seeds, :] = hid_ref[part]
        both_ref[seeds:, :] = hid_other_ref[part]

    @pl.when(lax.axis_index("rep") == 0)
    def _():
        run(own_ref, 0)

    @pl.when(lax.axis_index("rep") != 0)
    def _():
        run(mean_ref, 1)


def join_pairs(keep_ref, passed_ref, first_ref, *outs):
    for i, out_ref in enumerate((first_ref, *outs)):
        total = keep_ref[i] + passed_ref[i].astype(F32)
        out_ref[...] = total.astype(out_ref.dtype)


def total_gradients(sizes, first_ref, hid_near, hid_far, near, far, near_other, far_other, *rest):
    owners, seeds, f, fp, classes = sizes
    half = owners // 2
    blocks = rest[: half - 1]
    grad_w_ref, grad_v_ref, cot = rest[half - 1 :]
    width = first_ref.shape[1]
    split = seeds // 16
    piece = width // split
    block = near.shape[0] // half
    total = first_ref[...]
    for ref in blocks:
        total = total + ref[...].astype(F32)
    grad_w_ref[...] = total[:f]
    grad_v = None
    for hid, mine, other in ((hid_near, near, near_other), (hid_far, far, far_other)):
        for q in range(half):
            for p in range(split):
                at = slice(p * piece, p * piece + cot.shape[1])
                source = slice(q * block + fp, q * block + fp + 16)
                row = q * 2 * seeds + p * 16
                cot[row : row + 16, :] = mine[source, at]
                cot[row + seeds : row + seeds + 16, :] = other[source, at]
        part = lax.dot_general(cot[...], hid[...], OVER_FIRST, preferred_element_type=F32)
        grad_v = part if grad_v is None else grad_v + part
    grad_v_ref[...] = grad_v[:classes]


def place_gradients(w_mine, w_other, v_mine, v_other, ws_ref, wn_ref, vs_ref, vn_ref):
    @pl.when(lax.axis_index("rep") == 0)
    def _():
        ws_ref[...] = w_mine[...]
        wn_ref[...] = w_other[...]
        vs_ref[...] = v_mine[...]
        vn_ref[...] = v_other[...]

    @pl.when(lax.axis_index("rep") != 0)
    def _():
        ws_ref[...] = w_other[...]
        wn_ref[...] = w_mine[...]
        vs_ref[...] = v_other[...]
        vn_ref[...] = v_mine[...]


def swap(x):
    return lax.ppermute(x, "rep", [(0, 1), (1, 0)])


def shift_by(x, step, owners):
    return lax.ppermute(x, "feat", [(k, (k + step) % owners) for k in range(owners)])


def across(x, mask, owners):
    return lax.ppermute(x, "feat", [(k, k ^ mask) for k in range(owners)])


def gather_blocks(x, owners):
    mask = owners // 2
    while mask > 1:
        x = jnp.concatenate([x, across(x, mask, owners)], axis=0)
        mask //= 2
    return x, across(x, 1, owners)


def offsets_of(owners):
    offsets = [0]
    mask = owners // 2
    while mask:
        offsets = offsets + [o ^ mask for o in offsets]
        mask //= 2
    return tuple(offsets)


def on_device(
    seed_feat,
    hop_feat,
    frontier,
    nbr_index,
    hop_degree,
    seed_degree,
    w_self,
    w_neigh,
    v_self,
    v_neigh,
    cotangent,
):
    owners = lax.axis_size("feat")
    seeds, classes = cotangent.shape[1:]
    f, width = w_self.shape
    fan = hop_feat.shape[2]
    nodes = frontier.shape[2]
    hops = fan * seeds
    fp = up(f, 16)
    seed_rows = 16 * -(-(fp // 16) * seeds // hops)
    depth = owners * fp
    struct = jax.ShapeDtypeStruct

    message = call(
        functools.partial(weight_message, (seeds, f, fp, classes)),
        "weight_message",
        struct((fp + 16, width), BF16),
        [HBM] * 3,
        [pltpu.VMEM(cotangent.shape, BF16), pltpu.SemaphoreType.DMA((2,))],
        vmem=62,
    )(w_self, w_neigh, cotangent)
    far_mask = owners // 2
    fetched = across(message, far_mask, owners)
    lanes = up(f + 1, LANES)
    half = owners * seeds
    own_rows = fp + seed_rows
    keep, passed, rows, live = call(
        functools.partial(pack_features, (owners, seeds, fan, f, fp)),
        "pack_features",
        (
            struct((owners // 2, own_rows, hops), BF16),
            struct((owners // 2, own_rows, hops), BF16),
            struct((nodes + 8, lanes), F32),
            struct(nbr_index.shape[1:], jnp.int32),
        ),
        [HBM] * 5,
        [
            pltpu.VMEM(frontier.shape, BF16),
            pltpu.VMEM(hop_feat.shape, BF16),
            pltpu.VMEM((owners, own_rows, hops), BF16),
            pltpu.VMEM((half // LANES, f * fan, LANES), F32),
            pltpu.VMEM(seed_feat.shape, BF16),
            pltpu.VMEM((fp, half), F32),
            pltpu.VMEM(hop_degree.shape, jnp.int32),
            pltpu.VMEM(nbr_index.shape, jnp.int32),
            pltpu.SemaphoreType.DMA((5,)),
        ],
        micros=4,
    )(nbr_index, hop_degree, frontier, hop_feat, seed_feat)
    pairs = owners // 2
    passed = across(passed, 1, owners)
    fetched, live = lax.optimization_barrier((fetched, live))
    pieces = [message, fetched]
    mask = far_mask // 2
    while mask > 1:
        joined = jnp.concatenate(pieces, axis=0)
        joined, live = lax.optimization_barrier((joined, live))
        pieces = [joined, across(joined, mask, owners)]
        mask //= 2

    def gather(across_pair, begin, live, joined=()):
        outs = (struct((pairs // 2, fp, hops), BF16),)
        if joined:
            outs += (struct((2 * joined[0].shape[0], width), BF16),)
        return call(
            functools.partial(gather_means, (owners, seeds, fan, f, fp), across_pair, begin),
            "gather_means",
            outs,
            [SMEM] + [VMEM] * (1 + len(joined)),
            [pltpu.VMEM((hops, lanes), F32)],
            micros=MICROS,
        )(live, rows, *joined)

    def merge(keeps, passes):
        rows = keeps[0].shape[1]
        return list(
            call(
                functools.partial(merge_pairs, len(keeps)),
                "merge_pairs",
                (struct((2 * rows, hops), BF16),) * pairs,
                [VMEM] * (len(keeps) + len(passes)),
            )(*keeps, *passes)
        )

    def along(blocks, sign):
        return [blocks[0]] + [
            shift_by(blocks[k], sign * 2 * k, owners) for k in range(1, pairs)
        ]

    (low_passed,) = gather(True, 0, live)
    passed, low_passed = lax.optimization_barrier((passed, low_passed))
    merged = merge([keep], [passed])
    merged[0], live = lax.optimization_barrier((merged[0], live))
    own_blocks = along(merged, 1)
    (high_passed,) = gather(True, pairs // 2, live)
    high_passed, live = lax.optimization_barrier((high_passed, live))
    low_passed = across(low_passed, 1, owners)
    high_passed = across(high_passed, 1, owners)
    live, low_passed = lax.optimization_barrier((live, low_passed))
    (low,) = gather(False, 0, live)
    low, live, high_passed, *own_blocks = lax.optimization_barrier(
        [low, live, high_passed] + own_blocks
    )
    high, near = gather(False, pairs // 2, live, pieces)
    far = across(near, 1, owners)
    agg_blocks = along(merge([low, high], [low_passed, high_passed]), 1)
    far, agg_blocks[1] = lax.optimization_barrier((far, agg_blocks[1]))
    near_other, far_other = swap(near), swap(far)

    stacked = struct((depth, hops + LANES), BF16)
    own, mean, send = call(
        functools.partial(stack_features, (owners, seeds, fan, fp, seed_rows)),
        "stack_features",
        (stacked, stacked, stacked),
        [VMEM] * (owners + 1),
    )(seed_degree, *own_blocks, *agg_blocks)
    x_other = swap(send)
    logits, hidden, dpre = call(
        functools.partial(forward, (owners, seeds, fan, fp, width, offsets_of(owners))),
        "forward",
        (
            struct((1, seeds, classes), BF16),
            struct((2, seeds, width), BF16),
            struct((hops + LANES, width), BF16),
        ),
        [VMEM] * 10,
        [pltpu.VMEM((depth, width), BF16), pltpu.VMEM((depth, width), BF16)],
        micros=3,
    )(
        seed_degree,
        own,
        mean,
        near,
        far,
        near_other,
        far_other,
        v_self.T,
        v_neigh.T,
        cotangent,
    )
    keep, passed, both = call(
        functools.partial(products, (owners, seeds, fp)),
        "products",
        (
            struct((pairs, fp, width), F32),
            struct((pairs, fp, width), BF16),
            struct((2 * seeds, width), BF16),
        ),
        [VMEM] * 7,
        micros=2,
    )(own, mean, x_other, dpre, swap(dpre), hidden, swap(hidden))
    passed = across(passed, 1, owners)
    hid_near, hid_far = gather_blocks(both, owners)
    blocks = call(
        join_pairs,
        "join_pairs",
        (struct((fp, width), F32),) + (struct((fp, width), BF16),) * (pairs - 1),
        [VMEM] * 2,
    )(keep, passed)
    first, *blocks = along(blocks, -1)
    grad_w, grad_v = call(
        functools.partial(total_gradients, (owners, seeds, f, fp, classes)),
        "total_gradients",
        (struct((f, width), F32), struct((classes, width), F32)),
        [VMEM] * (6 + pairs),
        [pltpu.VMEM((owners * seeds, up(classes, LANES)), BF16)],
    )(first, hid_near, hid_far, near, far, near_other, far_other, *blocks)
    grads = call(
        place_gradients,
        "place_gradients",
        (struct((f, width), F32),) * 2 + (struct((classes, width), F32),) * 2,
        [VMEM] * 4,
    )(grad_w, swap(grad_w), grad_v, swap(grad_v))
    return (logits, grads[0], grads[1], grads[2].T, grads[3].T)


def solution(mesh):
    placed = (
        P(("groups", "rep"), "feat", None),
        P(("groups", "rep"), "feat", None, None),
        P(("groups", "rep"), "feat", None),
        P(("groups", "rep"), None, None, None),
        P(("groups", "rep"), None, None),
        P(("groups", "rep"), None),
        P("feat", None),
        P("feat", None),
        P(),
        P(),
        P(("groups", "rep"), "feat", None),
    )
    return jax.shard_map(
        on_device,
        mesh=mesh,
        in_specs=placed,
        out_specs=(
            P(("groups", "rep"), "feat", None),
            P(("groups", "feat"), None),
            P(("groups", "feat"), None),
            P("groups", None),
            P("groups", None),
        ),
        check_vma=False,
    )
```

```python
import functools

import jax
import jax.numpy as jnp
from jax import lax
from jax.experimental import pallas as pl
from jax.experimental.pallas import tpu as pltpu
from jax.sharding import PartitionSpec as P

F32 = jnp.float32
BF16 = jnp.bfloat16
LANES = 128
PACK = 56
FIRST = 62
VMEM = pl.BlockSpec(memory_space=pltpu.VMEM)
SMEM = pl.BlockSpec(memory_space=pltpu.SMEM)
HBM = pl.BlockSpec(memory_space=pltpu.HBM)
OVER_FIRST = (((0,), (0,)), ((), ()))
OVER_LAST = (((1,), (1,)), ((), ()))


def up(n, m):
    return -(-n // m) * m


def call(body, name, outs, in_specs, scratch=(), micros=1, vmem=40):
    return pl.pallas_call(
        body,
        name=name,
        out_shape=outs,
        in_specs=in_specs,
        out_specs=jax.tree.map(lambda _: VMEM, outs),
        scratch_shapes=list(scratch),
        compiler_params=pltpu.CompilerParams(vmem_limit_bytes=vmem << 20),
        cost_estimate=pl.CostEstimate(
            flops=0, bytes_accessed=int(micros * 3_000_000), transcendentals=0
        ),
    )


def mix_groups(pieces, seeds, towards):
    groups = LANES // seeds
    shape = next(p for p in pieces if p is not None).shape
    lane_group = lax.broadcasted_iota(jnp.int32, shape, 1) // seeds
    total = jnp.zeros(shape, F32)
    for k, piece in enumerate(pieces):
        if piece is None:
            continue
        turn = (k - towards) % groups
        moved = pltpu.roll(piece, turn * seeds, axis=1) if turn else piece
        total = jnp.where(lane_group == k, moved, total)
    return total


def weight_message(sizes, ws_ref, wn_ref, cot_ref, out_ref, cot, sems):
    seeds, f, fp, classes = sizes
    width = out_ref.shape[1]
    split = seeds // 16

    def fetch(ref):
        loads = (
            pltpu.make_async_copy(ref, out_ref.at[pl.ds(0, f), :], sems.at[0]),
            pltpu.make_async_copy(cot_ref, cot, sems.at[1]),
        )
        for load in loads:
            load.start()
        for load in loads:
            load.wait()

    @pl.when(lax.axis_index("rep") == 0)
    def _():
        fetch(ws_ref)

    @pl.when(lax.axis_index("rep") != 0)
    def _():
        fetch(wn_ref)

    if fp != f:
        out_ref[f:fp, :] = jnp.zeros((fp - f, width), BF16)
    out_ref[fp:, :] = jnp.zeros((16, width), BF16)
    for p in range(split):
        at = p * (width // split)
        out_ref[fp:, at : at + classes] = cot[0, p * 16 : (p + 1) * 16, :]


def pack_features(
    sizes,
    idx_ref,
    deg_ref,
    hop_ref,
    seed_ref,
    table_ref,
    keep_ref,
    pass_ref,
    live_ref,
    table,
    hop,
    packed,
    hop32,
    seed,
    seed32,
    deg,
    idx,
    sems,
):
    owners, seeds, fan, f, fp, nodes = sizes
    groups = LANES // seeds
    hops = fan * seeds
    loads = [
        pltpu.make_async_copy(source, target, sems.at[i])
        for i, (source, target) in enumerate(
            ((idx_ref, idx), (deg_ref, deg), (hop_ref, hop), (seed_ref, seed), (table_ref, table))
        )
    ]
    for load in loads:
        load.start()
    for load in loads[:4]:
        load.wait()
    tiles = owners * seeds // LANES
    for u in range(idx.shape[1]):
        live = jnp.where(deg[0] > u, idx[0, u], nodes)
        for tile in range(tiles):
            at = (u * tiles + tile) * fan
            live_ref[at : at + fan, :] = live[:, tile * LANES : (tile + 1) * LANES]
    if fp != f:
        packed[...] = jnp.zeros_like(packed)
        seed32[...] = jnp.zeros_like(seed32)
    for tile in range(owners // groups):
        at = slice(tile * LANES, (tile + 1) * LANES)
        hop32[tile] = hop[0, :, :, at].astype(F32).reshape(f * fan, LANES)
        for block in range(fan // groups):
            taken = [
                hop32[tile, pl.ds(block * groups + k, f, stride=fan), :] for k in range(groups)
            ]
            for e in range(groups):
                packed[tile * groups + e, :f, block * LANES : (block + 1) * LANES] = mix_groups(
                    taken, seeds, e
                ).astype(BF16)
    seed32[:f, :] = seed[0].astype(F32)
    bands = fp // 16
    for tile in range(owners // groups):
        at = slice(tile * LANES, (tile + 1) * LANES)
        for block in range(-(-bands // groups)):
            taken = [
                seed32[(block * groups + k) * 16 : (block * groups + k + 1) * 16, at]
                if block * groups + k < bands
                else None
                for k in range(groups)
            ]
            row, lane = divmod(block * LANES, hops)
            for e in range(groups):
                packed[
                    tile * groups + e, fp + row * 16 : fp + row * 16 + 16, lane : lane + LANES
                ] = mix_groups(taken, seeds, e).astype(BF16)

    side = lax.rem(lax.axis_index("feat"), 2)
    for j in range(owners // 2):
        owner = lax.rem(lax.axis_index("feat") // 2 + j, owners // 2)
        keep_ref[j] = packed[2 * owner + side]
        pass_ref[j] = packed[2 * owner + 1 - side]
    loads[4].wait()


def turn_table(f, table, rows):
    nodes = table.shape[2]
    step = 512 if nodes % 512 == 0 else LANES
    lanes = rows.shape[1]
    tail = (lax.broadcasted_iota(jnp.int32, (lanes - f, step), 0) == 0).astype(F32)

    def flip(i, _):
        at = pl.multiple_of(i * step, step)
        block = jnp.concatenate([table[0, :, pl.ds(at, step)].astype(F32), tail], axis=0)
        rows[pl.ds(at, step), :] = block.T
        return 0

    lax.fori_loop(0, nodes // step, flip, 0)
    rows[nodes:, :] = jnp.zeros((8, lanes), F32)


def gather_means(sizes, across_pair, steps, idx, rows, out_ref, picked):
    owners, seeds, fan, f, fp = sizes
    hops = out_ref.shape[2]
    groups = LANES // seeds
    tiles = owners * seeds // LANES
    slots = idx.shape[0] // (tiles * fan * LANES)
    me = lax.axis_index("feat")
    side = lax.rem(me, 2)
    if across_pair:
        side = 1 - side
    for i, step in enumerate(steps):
        owner = 2 * lax.rem(me // 2 + step, owners // 2) + side
        first = owner // groups * (fan * LANES) + lax.rem(owner, groups) * seeds

        def slot_step(t, _):
            src = first + t * LANES
            for k in range(seeds):
                total = rows[pl.ds(idx[src + k], 1), :]
                for u in range(1, slots):
                    at = src + (u * tiles * fan * LANES + k)
                    total = total + rows[pl.ds(idx[at], 1), :]
                picked[pl.ds(t * seeds + k, 1), :] = total
            return 0

        lax.fori_loop(0, fan, slot_step, 0)
        flat = picked[...].T
        mean = flat[:f] / flat[f : f + 1]
        if fp != f:
            mean = jnp.concatenate([mean, jnp.zeros((fp - f, hops), F32)], axis=0)
        out_ref[i] = mean.astype(BF16)


def join(first, second, joined):
    joined[: first.shape[0], :] = first[...]
    joined[first.shape[0] :, :] = second[...]


def merge_pairs(keep_ref, pass_ref, *rest):
    count, rows = keep_ref.shape[:2]
    outs = rest
    if len(rest) > count:
        join(rest[0], rest[1], rest[-1])
        outs = rest[2:-1]
    for i, out_ref in enumerate(outs):
        out_ref[:rows, :] = keep_ref[i]
        out_ref[rows:, :] = pass_ref[i]


def my_degrees(seed_degree_ref, seeds):
    half = seed_degree_ref.shape[1]
    wide = jnp.broadcast_to(seed_degree_ref[...], (8, half))
    shift = lax.rem(half - lax.axis_index("feat") * seeds, half)
    mine = pltpu.roll(wide, shift, axis=1)[:, :LANES]
    lane = lax.broadcasted_iota(jnp.int32, (8, LANES), 1)
    return jnp.where(lane < seeds, mine, 1)


def stack_features(sizes, seed_degree_ref, *rest):
    owners, seeds, fan, fp, seed_rows = sizes
    half = owners // 2
    own_blocks, agg_blocks = rest[:half], rest[half:owners]
    own_ref, mean_ref, send_ref = rest[owners:]
    groups = LANES // seeds
    hops = fan * seeds
    own_rows = fp + seed_rows
    lane = lax.broadcasted_iota(jnp.int32, (16, LANES), 1)
    for c in range(owners):
        ref, low = own_blocks[c // 2], c % 2 * own_rows
        own_ref[c * fp : (c + 1) * fp, :hops] = ref[low : low + fp, :]
        mean_ref[c * fp : (c + 1) * fp, :hops] = agg_blocks[c // 2][c % 2 * fp : (c % 2 + 1) * fp, :]
        for band in range(fp // 16):
            row, place = divmod(band * seeds, hops)
            tile = place // LANES
            row = low + fp + row * 16
            block = ref[row : row + 16, tile * LANES : (tile + 1) * LANES].astype(F32)
            turn = (-(band % groups)) % groups
            if turn:
                block = pltpu.roll(block, turn * seeds, axis=1)
            at = c * fp + band * 16
            own_ref[at : at + 16, hops:] = jnp.where(lane < seeds, block, 0.0).astype(BF16)
    degree = my_degrees(seed_degree_ref, seeds)[:1]
    node = lax.broadcasted_iota(jnp.int32, (hops, LANES), 0)
    seed = lax.broadcasted_iota(jnp.int32, (hops, LANES), 1)
    live = (node % seeds == seed) & (node // seeds < degree)
    total = jnp.dot(own_ref[:, :hops], live.astype(F32).astype(BF16), preferred_element_type=F32)
    mean_ref[:, hops:] = (total / degree.astype(F32)).astype(BF16)

    @pl.when(lax.axis_index("rep") == 0)
    def _():
        send_ref[...] = mean_ref[...]

    @pl.when(lax.axis_index("rep") != 0)
    def _():
        send_ref[...] = own_ref[...]


def forward(
    sizes,
    seed_degree_ref,
    own_ref,
    mean_ref,
    near_ref,
    far_ref,
    near_other_ref,
    far_other_ref,
    vs_ref,
    vn_ref,
    cot_ref,
    logits_ref,
    hidden_ref,
    dpre_ref,
    ws,
    wn,
):
    owners, seeds, fan, fp, width, offsets = sizes
    hops = fan * seeds
    half = owners // 2
    me = lax.axis_index("feat")
    block = near_ref.shape[0] // half

    def lay(near, far, w):
        for p, offset in enumerate(offsets):
            source = jnp.bitwise_xor(me, offset)
            c = 2 * lax.rem(me // 2 + half - source // 2, half) + offset % 2
            ref, q = (near, p) if p < half else (far, p - half)
            to = pl.ds(pl.multiple_of(c * fp, fp), fp)
            w[to, :] = ref[q * block : q * block + fp, :]

    @pl.when(lax.axis_index("rep") == 0)
    def _():
        lay(near_ref, far_ref, ws)
        lay(near_other_ref, far_other_ref, wn)

    @pl.when(lax.axis_index("rep") != 0)
    def _():
        lay(near_ref, far_ref, wn)
        lay(near_other_ref, far_other_ref, ws)

    pre = lax.dot_general(own_ref[...], ws[...], OVER_FIRST, preferred_element_type=F32)
    pre = pre + lax.dot_general(mean_ref[...], wn[...], OVER_FIRST, preferred_element_type=F32)
    pre = pre[: hops + seeds]
    sigma = jax.nn.sigmoid(pre)
    hidden = (pre * sigma).astype(BF16)
    slope = sigma * (1.0 + pre * (1.0 - sigma))
    degree = my_degrees(seed_degree_ref, seeds).astype(F32)
    degree = jnp.broadcast_to(degree[:1], (LANES, LANES)).T[:seeds]
    degree = jnp.concatenate([degree] * (width // LANES), axis=1)
    total = jnp.zeros((seeds, width), F32)
    for t in range(fan):
        row = hidden[t * seeds : (t + 1) * seeds].astype(F32)
        total = total + jnp.where(degree > t, row, 0.0)
    hidden_mean = (total / degree).astype(BF16)
    seed_hidden = hidden[hops:]
    hidden_ref[0] = seed_hidden
    hidden_ref[1] = hidden_mean
    logits = lax.dot_general(seed_hidden, vs_ref[...], OVER_LAST, preferred_element_type=F32)
    logits = logits + lax.dot_general(
        hidden_mean, vn_ref[...], OVER_LAST, preferred_element_type=F32
    )
    logits_ref[0] = logits.astype(BF16)
    cot = cot_ref[0]
    back_seed = jnp.dot(cot, vs_ref[...], preferred_element_type=F32)
    back_mean = jnp.dot(cot, vn_ref[...], preferred_element_type=F32)
    back_mean = back_mean / degree
    for t in range(fan):
        at = slice(t * seeds, (t + 1) * seeds)
        dpre_ref[at, :] = (jnp.where(degree > t, back_mean, 0.0) * slope[at]).astype(BF16)
    dpre_ref[hops : hops + seeds, :] = (back_seed * slope[hops:]).astype(BF16)
    dpre_ref[hops + seeds :, :] = jnp.zeros((LANES - seeds, width), BF16)


def products(
    sizes,
    own_ref,
    mean_ref,
    x_ref,
    dpre_ref,
    dpre_other_ref,
    hid_ref,
    hid_other_ref,
    keep_ref,
    pass_ref,
    both_ref,
):
    owners, seeds, fp = sizes

    def run(mine_ref, part):
        total = jnp.dot(mine_ref[...], dpre_ref[...], preferred_element_type=F32)
        total = total + jnp.dot(x_ref[...], dpre_other_ref[...], preferred_element_type=F32)
        for c in range(owners):
            block = total[c * fp : (c + 1) * fp]
            if c % 2:
                pass_ref[c // 2] = block.astype(BF16)
            else:
                keep_ref[c // 2] = block
        both_ref[:seeds, :] = hid_ref[part]
        both_ref[seeds:, :] = hid_other_ref[part]

    @pl.when(lax.axis_index("rep") == 0)
    def _():
        run(own_ref, 0)

    @pl.when(lax.axis_index("rep") != 0)
    def _():
        run(mean_ref, 1)


def join_pairs(keep_ref, passed_ref, first_ref, *outs):
    for i, out_ref in enumerate((first_ref, *outs)):
        total = keep_ref[i] + passed_ref[i].astype(F32)
        out_ref[...] = total.astype(out_ref.dtype)


def total_gradients(sizes, first_ref, hid_near, hid_far, near, far, near_other, far_other, *rest):
    owners, seeds, f, fp, classes = sizes
    half = owners // 2
    blocks = rest[: half - 1]
    grad_w_ref, grad_v_ref, cot = rest[half - 1 :]
    width = first_ref.shape[1]
    split = seeds // 16
    piece = width // split
    block = near.shape[0] // half
    total = first_ref[...]
    for ref in blocks:
        total = total + ref[...].astype(F32)
    grad_w_ref[...] = total[:f]
    grad_v = None
    for hid, mine, other in ((hid_near, near, near_other), (hid_far, far, far_other)):
        for q in range(half):
            for p in range(split):
                at = slice(p * piece, p * piece + cot.shape[1])
                source = slice(q * block + fp, q * block + fp + 16)
                row = q * 2 * seeds + p * 16
                cot[row : row + 16, :] = mine[source, at]
                cot[row + seeds : row + seeds + 16, :] = other[source, at]
        part = lax.dot_general(cot[...], hid[...], OVER_FIRST, preferred_element_type=F32)
        grad_v = part if grad_v is None else grad_v + part
    grad_v_ref[...] = grad_v[:classes]


def place_gradients(w_mine, w_other, v_mine, v_other, ws_ref, wn_ref, vs_ref, vn_ref):
    @pl.when(lax.axis_index("rep") == 0)
    def _():
        ws_ref[...] = w_mine[...]
        wn_ref[...] = w_other[...]
        vs_ref[...] = v_mine[...]
        vn_ref[...] = v_other[...]

    @pl.when(lax.axis_index("rep") != 0)
    def _():
        ws_ref[...] = w_other[...]
        wn_ref[...] = w_mine[...]
        vs_ref[...] = v_other[...]
        vn_ref[...] = v_mine[...]


def swap(x):
    return lax.ppermute(x, "rep", [(0, 1), (1, 0)])


def shift_by(x, step, owners):
    return lax.ppermute(x, "feat", [(k, (k + step) % owners) for k in range(owners)])


def across(x, mask, owners):
    return lax.ppermute(x, "feat", [(k, k ^ mask) for k in range(owners)])


def join_rows(first, second):
    rows, columns = first.shape
    return call(
        join, "join_rows", jax.ShapeDtypeStruct((2 * rows, columns), first.dtype), [VMEM] * 2
    )(first, second)


def gather_blocks(x, owners):
    mask = owners // 2
    while mask > 1:
        x = join_rows(x, across(x, mask, owners))
        mask //= 2
    return x, across(x, 1, owners)


def offsets_of(owners):
    offsets = [0]
    mask = owners // 2
    while mask:
        offsets = offsets + [o ^ mask for o in offsets]
        mask //= 2
    return tuple(offsets)


def on_device(
    seed_feat,
    hop_feat,
    frontier,
    nbr_index,
    hop_degree,
    seed_degree,
    w_self,
    w_neigh,
    v_self,
    v_neigh,
    cotangent,
):
    owners = lax.axis_size("feat")
    seeds, classes = cotangent.shape[1:]
    f, width = w_self.shape
    fan = hop_feat.shape[2]
    nodes = frontier.shape[2]
    hops = fan * seeds
    fp = up(f, 16)
    seed_rows = 16 * -(-(fp // 16) * seeds // hops)
    depth = owners * fp
    struct = jax.ShapeDtypeStruct

    message = call(
        functools.partial(weight_message, (seeds, f, fp, classes)),
        "weight_message",
        struct((fp + 16, width), BF16),
        [HBM] * 3,
        [pltpu.VMEM(cotangent.shape, BF16), pltpu.SemaphoreType.DMA((2,))],
        vmem=FIRST,
    )(w_self, w_neigh, cotangent)
    far_mask = owners // 2
    fetched = across(message, far_mask, owners)
    lanes = up(f + 1, LANES)
    half = owners * seeds
    own_rows = fp + seed_rows
    keep, passed, live, table = call(
        functools.partial(pack_features, (owners, seeds, fan, f, fp, nodes)),
        "pack_features",
        (
            struct((owners // 2, own_rows, hops), BF16),
            struct((owners // 2, own_rows, hops), BF16),
            struct((nbr_index.size // LANES, LANES), jnp.int32),
            struct(frontier.shape, BF16),
        ),
        [HBM] * 5,
        [
            pltpu.VMEM(hop_feat.shape, BF16),
            pltpu.VMEM((owners, own_rows, hops), BF16),
            pltpu.VMEM((half // LANES, f * fan, LANES), F32),
            pltpu.VMEM(seed_feat.shape, BF16),
            pltpu.VMEM((fp, half), F32),
            pltpu.VMEM(hop_degree.shape, jnp.int32),
            pltpu.VMEM(nbr_index.shape, jnp.int32),
            pltpu.SemaphoreType.DMA((5,)),
        ],
        vmem=PACK,
    )(nbr_index, hop_degree, hop_feat, seed_feat, frontier)
    rows = call(
        functools.partial(turn_table, f),
        "turn_table",
        struct((nodes + 8, lanes), F32),
        [VMEM],
    )(table)
    live = live.reshape(-1)
    pairs = owners // 2
    passed = across(passed, 1, owners)
    fetched, live, rows = lax.optimization_barrier((fetched, live, rows))
    pieces = [message, fetched]
    mask = far_mask // 2
    while mask > 1:
        joined = join_rows(*pieces)
        joined, live = lax.optimization_barrier((joined, live))
        pieces = [joined, across(joined, mask, owners)]
        mask //= 2

    def gather(across_pair, steps, live):
        return call(
            functools.partial(gather_means, (owners, seeds, fan, f, fp), across_pair, steps),
            "gather_means",
            struct((len(steps), fp, hops), BF16),
            [SMEM, VMEM],
            [pltpu.VMEM((hops, lanes), F32)],
        )(live, rows)

    def merge(keep, passed, pieces=()):
        count, rows = keep.shape[:2]
        outs = (struct((2 * rows, hops), BF16),) * count
        if pieces:
            outs += (struct((2 * pieces[0].shape[0], width), BF16),)
        return list(
            call(merge_pairs, "merge_pairs", outs, [VMEM] * (2 + len(pieces)))(
                keep, passed, *pieces
            )
        )

    def along(blocks, sign, steps):
        return [
            shift_by(x, sign * 2 * k, owners) if k else x for k, x in zip(steps, blocks)
        ]

    order = sorted(range(1, pairs), key=lambda k: (-min(k, pairs - k), k)) + [0]
    early, late = order[: pairs // 2], order[pairs // 2 :]
    early_passed = gather(True, early, live)
    passed, early_passed = lax.optimization_barrier((passed, early_passed))
    *merged, near = merge(keep, passed, pieces)
    merged[0], live = lax.optimization_barrier((merged[0], live))
    own_blocks = along(merged, 1, range(pairs))
    far = across(near, 1, owners)
    early_passed = across(early_passed, 1, owners)
    late_passed = gather(True, late, live)
    late_passed, live = lax.optimization_barrier((late_passed, live))
    late_passed = across(late_passed, 1, owners)
    live, early_passed = lax.optimization_barrier((live, early_passed))
    means = gather(False, early, live)
    merged = merge(means, early_passed)
    merged[0], live, near, far, *own_blocks = lax.optimization_barrier(
        [merged[0], live, near, far] + own_blocks
    )
    agg_blocks = dict(zip(early, along(merged, 1, early)))
    means = gather(False, late, live)
    near_other, far_other = swap(near), swap(far)
    means, near_other, far_other = lax.optimization_barrier((means, near_other, far_other))
    agg_blocks |= dict(zip(late, along(merge(means, late_passed), 1, late)))
    agg_blocks = [agg_blocks[k] for k in range(pairs)]

    stacked = struct((depth, hops + LANES), BF16)
    own, mean, send = call(
        functools.partial(stack_features, (owners, seeds, fan, fp, seed_rows)),
        "stack_features",
        (stacked, stacked, stacked),
        [VMEM] * (owners + 1),
    )(seed_degree, *own_blocks, *agg_blocks)
    x_other = swap(send)
    logits, hidden, dpre = call(
        functools.partial(forward, (owners, seeds, fan, fp, width, offsets_of(owners))),
        "forward",
        (
            struct((1, seeds, classes), BF16),
            struct((2, seeds, width), BF16),
            struct((hops + LANES, width), BF16),
        ),
        [VMEM] * 10,
        [pltpu.VMEM((depth, width), BF16), pltpu.VMEM((depth, width), BF16)],
        micros=3,
    )(
        seed_degree,
        own,
        mean,
        near,
        far,
        near_other,
        far_other,
        v_self.T,
        v_neigh.T,
        cotangent,
    )
    keep, passed, both = call(
        functools.partial(products, (owners, seeds, fp)),
        "products",
        (
            struct((pairs, fp, width), F32),
            struct((pairs, fp, width), BF16),
            struct((2 * seeds, width), BF16),
        ),
        [VMEM] * 7,
        micros=2,
    )(own, mean, x_other, dpre, swap(dpre), hidden, swap(hidden))
    passed = across(passed, 1, owners)
    hid_near, hid_far = gather_blocks(both, owners)
    blocks = call(
        join_pairs,
        "join_pairs",
        (struct((fp, width), F32),) + (struct((fp, width), BF16),) * (pairs - 1),
        [VMEM] * 2,
    )(keep, passed)
    first, *blocks = along(blocks, -1, range(pairs))
    grad_w, grad_v = call(
        functools.partial(total_gradients, (owners, seeds, f, fp, classes)),
        "total_gradients",
        (struct((f, width), F32), struct((classes, width), F32)),
        [VMEM] * (6 + pairs),
        [pltpu.VMEM((owners * seeds, up(classes, LANES)), BF16)],
    )(first, hid_near, hid_far, near, far, near_other, far_other, *blocks)
    grads = call(
        place_gradients,
        "place_gradients",
        (struct((f, width), F32),) * 2 + (struct((classes, width), F32),) * 2,
        [VMEM] * 4,
    )(grad_w, swap(grad_w), grad_v, swap(grad_v))
    return (logits, grads[0], grads[1], grads[2].T, grads[3].T)


def solution(mesh):
    placed = (
        P(("groups", "rep"), "feat", None),
        P(("groups", "rep"), "feat", None, None),
        P(("groups", "rep"), "feat", None),
        P(("groups", "rep"), None, None, None),
        P(("groups", "rep"), None, None),
        P(("groups", "rep"), None),
        P("feat", None),
        P("feat", None),
        P(),
        P(),
        P(("groups", "rep"), "feat", None),
    )
    return jax.shard_map(
        on_device,
        mesh=mesh,
        in_specs=placed,
        out_specs=(
            P(("groups", "rep"), "feat", None),
            P(("groups", "feat"), None),
            P(("groups", "feat"), None),
            P("groups", None),
            P("groups", None),
        ),
        check_vma=False,
    )
```

```python
import functools

import jax
import jax.numpy as jnp
from jax import lax
from jax.experimental import pallas as pl
from jax.experimental.pallas import tpu as pltpu
from jax.sharding import PartitionSpec as P

F32 = jnp.float32
BF16 = jnp.bfloat16
LANES = 128
PACK = 56
FIRST = 62
VMEM = pl.BlockSpec(memory_space=pltpu.VMEM)
SMEM = pl.BlockSpec(memory_space=pltpu.SMEM)
HBM = pl.BlockSpec(memory_space=pltpu.HBM)
OVER_FIRST = (((0,), (0,)), ((), ()))
OVER_LAST = (((1,), (1,)), ((), ()))


def up(n, m):
    return -(-n // m) * m


def call(body, name, outs, in_specs, scratch=(), micros=1, vmem=40):
    return pl.pallas_call(
        body,
        name=name,
        out_shape=outs,
        in_specs=in_specs,
        out_specs=jax.tree.map(lambda _: VMEM, outs),
        scratch_shapes=list(scratch),
        compiler_params=pltpu.CompilerParams(vmem_limit_bytes=vmem << 20),
        cost_estimate=pl.CostEstimate(
            flops=0, bytes_accessed=int(micros * 3_000_000), transcendentals=0
        ),
    )


def mix_groups(pieces, seeds, towards):
    groups = LANES // seeds
    shape = next(p for p in pieces if p is not None).shape
    lane_group = lax.broadcasted_iota(jnp.int32, shape, 1) // seeds
    total = jnp.zeros(shape, F32)
    for k, piece in enumerate(pieces):
        if piece is None:
            continue
        turn = (k - towards) % groups
        moved = pltpu.roll(piece, turn * seeds, axis=1) if turn else piece
        total = jnp.where(lane_group == k, moved, total)
    return total


def weight_message(sizes, ws_ref, wn_ref, cot_ref, out_ref, cot, sems):
    seeds, f, fp, classes = sizes
    width = out_ref.shape[1]
    split = seeds // 16

    def fetch(ref):
        loads = (
            pltpu.make_async_copy(ref, out_ref.at[pl.ds(0, f), :], sems.at[0]),
            pltpu.make_async_copy(cot_ref, cot, sems.at[1]),
        )
        for load in loads:
            load.start()
        for load in loads:
            load.wait()

    @pl.when(lax.axis_index("rep") == 0)
    def _():
        fetch(ws_ref)

    @pl.when(lax.axis_index("rep") != 0)
    def _():
        fetch(wn_ref)

    if fp != f:
        out_ref[f:fp, :] = jnp.zeros((fp - f, width), BF16)
    out_ref[fp:, :] = jnp.zeros((16, width), BF16)
    for p in range(split):
        at = p * (width // split)
        out_ref[fp:, at : at + classes] = cot[0, p * 16 : (p + 1) * 16, :]


def pack_features(
    sizes,
    idx_ref,
    deg_ref,
    hop_ref,
    seed_ref,
    table_ref,
    keep_ref,
    pass_ref,
    live_ref,
    table,
    hop,
    packed,
    hop32,
    seed,
    seed32,
    deg,
    idx,
    sems,
):
    owners, seeds, fan, f, fp, nodes = sizes
    groups = LANES // seeds
    hops = fan * seeds
    loads = [
        pltpu.make_async_copy(source, target, sems.at[i])
        for i, (source, target) in enumerate(
            ((idx_ref, idx), (deg_ref, deg), (hop_ref, hop), (seed_ref, seed), (table_ref, table))
        )
    ]
    for load in loads:
        load.start()
    for load in loads[:4]:
        load.wait()
    tiles = owners * seeds // LANES
    for u in range(idx.shape[1]):
        live = jnp.where(deg[0] > u, idx[0, u], nodes)
        for tile in range(tiles):
            at = (u * tiles + tile) * fan
            live_ref[at : at + fan, :] = live[:, tile * LANES : (tile + 1) * LANES]
    if fp != f:
        packed[...] = jnp.zeros_like(packed)
        seed32[...] = jnp.zeros_like(seed32)
    for tile in range(owners // groups):
        at = slice(tile * LANES, (tile + 1) * LANES)
        hop32[tile] = hop[0, :, :, at].astype(F32).reshape(f * fan, LANES)
        for block in range(fan // groups):
            taken = [
                hop32[tile, pl.ds(block * groups + k, f, stride=fan), :] for k in range(groups)
            ]
            for e in range(groups):
                packed[tile * groups + e, :f, block * LANES : (block + 1) * LANES] = mix_groups(
                    taken, seeds, e
                ).astype(BF16)
    seed32[:f, :] = seed[0].astype(F32)
    bands = fp // 16
    for tile in range(owners // groups):
        at = slice(tile * LANES, (tile + 1) * LANES)
        for block in range(-(-bands // groups)):
            taken = [
                seed32[(block * groups + k) * 16 : (block * groups + k + 1) * 16, at]
                if block * groups + k < bands
                else None
                for k in range(groups)
            ]
            row, lane = divmod(block * LANES, hops)
            for e in range(groups):
                packed[
                    tile * groups + e, fp + row * 16 : fp + row * 16 + 16, lane : lane + LANES
                ] = mix_groups(taken, seeds, e).astype(BF16)

    side = lax.rem(lax.axis_index("feat"), 2)
    for j in range(owners // 2):
        owner = lax.rem(lax.axis_index("feat") // 2 + j, owners // 2)
        keep_ref[j] = packed[2 * owner + side]
        pass_ref[j] = packed[2 * owner + 1 - side]
    loads[4].wait()


def turn_table(f, table, rows):
    nodes = table.shape[2]
    step = 512 if nodes % 512 == 0 else LANES
    lanes = rows.shape[1]
    tail = (lax.broadcasted_iota(jnp.int32, (lanes - f, step), 0) == 0).astype(F32)

    def flip(i, _):
        at = pl.multiple_of(i * step, step)
        block = jnp.concatenate([table[0, :, pl.ds(at, step)].astype(F32), tail], axis=0)
        rows[pl.ds(at, step), :] = block.T
        return 0

    lax.fori_loop(0, nodes // step, flip, 0)
    rows[nodes:, :] = jnp.zeros((8, lanes), F32)


def gather_means(sizes, across_pair, steps, idx, rows, out_ref, picked):
    owners, seeds, fan, f, fp = sizes
    hops = out_ref.shape[2]
    groups = LANES // seeds
    tiles = owners * seeds // LANES
    slots = idx.shape[0] // (tiles * fan * LANES)
    me = lax.axis_index("feat")
    side = lax.rem(me, 2)
    if across_pair:
        side = 1 - side
    for i, step in enumerate(steps):
        owner = 2 * lax.rem(me // 2 + step, owners // 2) + side
        first = owner // groups * (fan * LANES) + lax.rem(owner, groups) * seeds

        def slot_step(t, _):
            src = first + t * LANES
            for k in range(seeds):
                total = rows[pl.ds(idx[src + k], 1), :]
                for u in range(1, slots):
                    at = src + (u * tiles * fan * LANES + k)
                    total = total + rows[pl.ds(idx[at], 1), :]
                picked[pl.ds(t * seeds + k, 1), :] = total
            return 0

        lax.fori_loop(0, fan, slot_step, 0)
        flat = picked[...].T
        mean = flat[:f] / flat[f : f + 1]
        if fp != f:
            mean = jnp.concatenate([mean, jnp.zeros((fp - f, hops), F32)], axis=0)
        out_ref[i] = mean.astype(BF16)


def join(first, second, joined):
    joined[: first.shape[0], :] = first[...]
    joined[first.shape[0] :, :] = second[...]


def merge_pairs(keep_ref, pass_ref, *rest):
    count, rows = keep_ref.shape[:2]
    outs = rest
    if len(rest) > count:
        join(rest[0], rest[1], rest[-1])
        outs = rest[2:-1]
    for i, out_ref in enumerate(outs):
        out_ref[:rows, :] = keep_ref[i]
        out_ref[rows:, :] = pass_ref[i]


def my_degrees(seed_degree_ref, seeds):
    half = seed_degree_ref.shape[1]
    wide = jnp.broadcast_to(seed_degree_ref[...], (8, half))
    shift = lax.rem(half - lax.axis_index("feat") * seeds, half)
    mine = pltpu.roll(wide, shift, axis=1)[:, :LANES]
    lane = lax.broadcasted_iota(jnp.int32, (8, LANES), 1)
    return jnp.where(lane < seeds, mine, 1)


def stack_features(sizes, seed_degree_ref, *rest):
    owners, seeds, fan, fp, seed_rows = sizes
    half = owners // 2
    own_blocks, agg_blocks = rest[:half], rest[half:owners]
    own_ref, mean_ref, send_ref = rest[owners:]
    groups = LANES // seeds
    hops = fan * seeds
    own_rows = fp + seed_rows
    lane = lax.broadcasted_iota(jnp.int32, (16, LANES), 1)
    for c in range(owners):
        ref, low = own_blocks[c // 2], c % 2 * own_rows
        own_ref[c * fp : (c + 1) * fp, :hops] = ref[low : low + fp, :]
        mean_ref[c * fp : (c + 1) * fp, :hops] = agg_blocks[c // 2][c % 2 * fp : (c % 2 + 1) * fp, :]
        for band in range(fp // 16):
            row, place = divmod(band * seeds, hops)
            tile = place // LANES
            row = low + fp + row * 16
            block = ref[row : row + 16, tile * LANES : (tile + 1) * LANES].astype(F32)
            turn = (-(band % groups)) % groups
            if turn:
                block = pltpu.roll(block, turn * seeds, axis=1)
            at = c * fp + band * 16
            own_ref[at : at + 16, hops:] = jnp.where(lane < seeds, block, 0.0).astype(BF16)
    degree = my_degrees(seed_degree_ref, seeds)[:1]
    node = lax.broadcasted_iota(jnp.int32, (hops, LANES), 0)
    seed = lax.broadcasted_iota(jnp.int32, (hops, LANES), 1)
    live = (node % seeds == seed) & (node // seeds < degree)
    total = jnp.dot(own_ref[:, :hops], live.astype(F32).astype(BF16), preferred_element_type=F32)
    mean_ref[:, hops:] = (total / degree.astype(F32)).astype(BF16)

    @pl.when(lax.axis_index("rep") == 0)
    def _():
        send_ref[...] = mean_ref[...]

    @pl.when(lax.axis_index("rep") != 0)
    def _():
        send_ref[...] = own_ref[...]


def forward(
    sizes,
    seed_degree_ref,
    own_ref,
    mean_ref,
    near_ref,
    far_ref,
    near_other_ref,
    far_other_ref,
    vs_ref,
    vn_ref,
    cot_ref,
    logits_ref,
    hidden_ref,
    dpre_ref,
    ws,
    wn,
):
    owners, seeds, fan, fp, width, offsets = sizes
    hops = fan * seeds
    half = owners // 2
    me = lax.axis_index("feat")
    block = near_ref.shape[0] // half

    def lay(near, far, w):
        for p, offset in enumerate(offsets):
            source = jnp.bitwise_xor(me, offset)
            c = 2 * lax.rem(me // 2 + half - source // 2, half) + offset % 2
            ref, q = (near, p) if p < half else (far, p - half)
            to = pl.ds(pl.multiple_of(c * fp, fp), fp)
            w[to, :] = ref[q * block : q * block + fp, :]

    @pl.when(lax.axis_index("rep") == 0)
    def _():
        lay(near_ref, far_ref, ws)
        lay(near_other_ref, far_other_ref, wn)

    @pl.when(lax.axis_index("rep") != 0)
    def _():
        lay(near_ref, far_ref, wn)
        lay(near_other_ref, far_other_ref, ws)

    pre = lax.dot_general(own_ref[...], ws[...], OVER_FIRST, preferred_element_type=F32)
    pre = pre + lax.dot_general(mean_ref[...], wn[...], OVER_FIRST, preferred_element_type=F32)
    pre = pre[: hops + seeds]
    sigma = jax.nn.sigmoid(pre)
    hidden = (pre * sigma).astype(BF16)
    slope = sigma * (1.0 + pre * (1.0 - sigma))
    degree = my_degrees(seed_degree_ref, seeds).astype(F32)
    degree = jnp.broadcast_to(degree[:1], (LANES, LANES)).T[:seeds]
    degree = jnp.concatenate([degree] * (width // LANES), axis=1)
    total = jnp.zeros((seeds, width), F32)
    for t in range(fan):
        row = hidden[t * seeds : (t + 1) * seeds].astype(F32)
        total = total + jnp.where(degree > t, row, 0.0)
    hidden_mean = (total / degree).astype(BF16)
    seed_hidden = hidden[hops:]
    hidden_ref[0] = seed_hidden
    hidden_ref[1] = hidden_mean
    logits = lax.dot_general(seed_hidden, vs_ref[...], OVER_LAST, preferred_element_type=F32)
    logits = logits + lax.dot_general(
        hidden_mean, vn_ref[...], OVER_LAST, preferred_element_type=F32
    )
    logits_ref[0] = logits.astype(BF16)
    cot = cot_ref[0]
    back_seed = jnp.dot(cot, vs_ref[...], preferred_element_type=F32)
    back_mean = jnp.dot(cot, vn_ref[...], preferred_element_type=F32)
    back_mean = back_mean / degree
    for t in range(fan):
        at = slice(t * seeds, (t + 1) * seeds)
        dpre_ref[at, :] = (jnp.where(degree > t, back_mean, 0.0) * slope[at]).astype(BF16)
    dpre_ref[hops : hops + seeds, :] = (back_seed * slope[hops:]).astype(BF16)
    dpre_ref[hops + seeds :, :] = jnp.zeros((LANES - seeds, width), BF16)


def products(
    sizes,
    own_ref,
    mean_ref,
    x_ref,
    dpre_ref,
    dpre_other_ref,
    hid_ref,
    hid_other_ref,
    keep_ref,
    pass_ref,
    both_ref,
):
    owners, seeds, fp = sizes

    def run(mine_ref, part):
        total = jnp.dot(mine_ref[...], dpre_ref[...], preferred_element_type=F32)
        total = total + jnp.dot(x_ref[...], dpre_other_ref[...], preferred_element_type=F32)
        for c in range(owners):
            block = total[c * fp : (c + 1) * fp]
            if c % 2:
                pass_ref[c // 2] = block.astype(BF16)
            else:
                keep_ref[c // 2] = block
        both_ref[:seeds, :] = hid_ref[part]
        both_ref[seeds:, :] = hid_other_ref[part]

    @pl.when(lax.axis_index("rep") == 0)
    def _():
        run(own_ref, 0)

    @pl.when(lax.axis_index("rep") != 0)
    def _():
        run(mean_ref, 1)


def join_pairs(keep_ref, passed_ref, first_ref, *outs):
    for i, out_ref in enumerate((first_ref, *outs)):
        total = keep_ref[i] + passed_ref[i].astype(F32)
        out_ref[...] = total.astype(out_ref.dtype)


def total_gradients(sizes, first_ref, hid_near, hid_far, near, far, near_other, far_other, *rest):
    owners, seeds, f, fp, classes = sizes
    half = owners // 2
    blocks = rest[: half - 1]
    grad_w_ref, grad_v_ref, cot = rest[half - 1 :]
    width = first_ref.shape[1]
    split = seeds // 16
    piece = width // split
    block = near.shape[0] // half
    total = first_ref[...]
    for ref in blocks:
        total = total + ref[...].astype(F32)
    grad_w_ref[...] = total[:f]
    grad_v = None
    for hid, mine, other in ((hid_near, near, near_other), (hid_far, far, far_other)):
        for q in range(half):
            for p in range(split):
                at = slice(p * piece, p * piece + cot.shape[1])
                source = slice(q * block + fp, q * block + fp + 16)
                row = q * 2 * seeds + p * 16
                cot[row : row + 16, :] = mine[source, at]
                cot[row + seeds : row + seeds + 16, :] = other[source, at]
        part = lax.dot_general(cot[...], hid[...], OVER_FIRST, preferred_element_type=F32)
        grad_v = part if grad_v is None else grad_v + part
    grad_v_ref[...] = grad_v[:classes]


def place_gradients(w_mine, w_other, v_mine, v_other, ws_ref, wn_ref, vs_ref, vn_ref):
    @pl.when(lax.axis_index("rep") == 0)
    def _():
        ws_ref[...] = w_mine[...]
        wn_ref[...] = w_other[...]
        vs_ref[...] = v_mine[...]
        vn_ref[...] = v_other[...]

    @pl.when(lax.axis_index("rep") != 0)
    def _():
        ws_ref[...] = w_other[...]
        wn_ref[...] = w_mine[...]
        vs_ref[...] = v_other[...]
        vn_ref[...] = v_mine[...]


def swap(x):
    return lax.ppermute(x, "rep", [(0, 1), (1, 0)])


def shift_by(x, step, owners):
    return lax.ppermute(x, "feat", [(k, (k + step) % owners) for k in range(owners)])


def across(x, mask, owners):
    return lax.ppermute(x, "feat", [(k, k ^ mask) for k in range(owners)])


def join_rows(first, second):
    rows, columns = first.shape
    return call(
        join, "join_rows", jax.ShapeDtypeStruct((2 * rows, columns), first.dtype), [VMEM] * 2
    )(first, second)


def gather_blocks(x, owners):
    mask = owners // 2
    while mask > 1:
        x = join_rows(x, across(x, mask, owners))
        mask //= 2
    return x, across(x, 1, owners)


def offsets_of(owners):
    offsets = [0]
    mask = owners // 2
    while mask:
        offsets = offsets + [o ^ mask for o in offsets]
        mask //= 2
    return tuple(offsets)


def on_device(
    seed_feat,
    hop_feat,
    frontier,
    nbr_index,
    hop_degree,
    seed_degree,
    w_self,
    w_neigh,
    v_self,
    v_neigh,
    cotangent,
):
    owners = lax.axis_size("feat")
    seeds, classes = cotangent.shape[1:]
    f, width = w_self.shape
    fan = hop_feat.shape[2]
    nodes = frontier.shape[2]
    hops = fan * seeds
    fp = up(f, 16)
    seed_rows = 16 * -(-(fp // 16) * seeds // hops)
    depth = owners * fp
    struct = jax.ShapeDtypeStruct

    message = call(
        functools.partial(weight_message, (seeds, f, fp, classes)),
        "weight_message",
        struct((fp + 16, width), BF16),
        [HBM] * 3,
        [pltpu.VMEM(cotangent.shape, BF16), pltpu.SemaphoreType.DMA((2,))],
        vmem=FIRST,
    )(w_self, w_neigh, cotangent)
    far_mask = owners // 2
    fetched = across(message, far_mask, owners)
    lanes = up(f + 1, LANES)
    half = owners * seeds
    own_rows = fp + seed_rows
    keep, passed, live, table = call(
        functools.partial(pack_features, (owners, seeds, fan, f, fp, nodes)),
        "pack_features",
        (
            struct((owners // 2, own_rows, hops), BF16),
            struct((owners // 2, own_rows, hops), BF16),
            struct((nbr_index.size // LANES, LANES), jnp.int32),
            struct(frontier.shape, BF16),
        ),
        [HBM] * 5,
        [
            pltpu.VMEM(hop_feat.shape, BF16),
            pltpu.VMEM((owners, own_rows, hops), BF16),
            pltpu.VMEM((half // LANES, f * fan, LANES), F32),
            pltpu.VMEM(seed_feat.shape, BF16),
            pltpu.VMEM((fp, half), F32),
            pltpu.VMEM(hop_degree.shape, jnp.int32),
            pltpu.VMEM(nbr_index.shape, jnp.int32),
            pltpu.SemaphoreType.DMA((5,)),
        ],
        vmem=PACK,
    )(nbr_index, hop_degree, hop_feat, seed_feat, frontier)
    rows = call(
        functools.partial(turn_table, f),
        "turn_table",
        struct((nodes + 8, lanes), F32),
        [VMEM],
    )(table)
    live = live.reshape(-1)
    pairs = owners // 2
    passed = across(passed, 1, owners)
    fetched, live, rows = lax.optimization_barrier((fetched, live, rows))
    pieces = [message, fetched]
    mask = far_mask // 2
    while mask > 1:
        joined = join_rows(*pieces)
        joined, live = lax.optimization_barrier((joined, live))
        pieces = [joined, across(joined, mask, owners)]
        mask //= 2

    def gather(across_pair, steps, live):
        return call(
            functools.partial(gather_means, (owners, seeds, fan, f, fp), across_pair, steps),
            "gather_means",
            struct((len(steps), fp, hops), BF16),
            [SMEM, VMEM],
            [pltpu.VMEM((hops, lanes), F32)],
        )(live, rows)

    def merge(keep, passed, pieces=()):
        count, rows = keep.shape[:2]
        outs = (struct((2 * rows, hops), BF16),) * count
        if pieces:
            outs += (struct((2 * pieces[0].shape[0], width), BF16),)
        return list(
            call(merge_pairs, "merge_pairs", outs, [VMEM] * (2 + len(pieces)))(
                keep, passed, *pieces
            )
        )

    def along(blocks, sign, steps):
        return [
            shift_by(x, sign * 2 * k, owners) if k else x for k, x in zip(steps, blocks)
        ]

    order = sorted(range(1, pairs), key=lambda k: (-min(k, pairs - k), k)) + [0]
    early, late = order[: pairs // 2], order[pairs // 2 :]
    early_passed = gather(True, early, live)
    passed, early_passed = lax.optimization_barrier((passed, early_passed))
    merged = merge(keep, passed)
    merged[0], live = lax.optimization_barrier((merged[0], live))
    own_blocks = along(merged, 1, range(pairs))
    early_passed = across(early_passed, 1, owners)
    late_passed = gather(True, late, live)
    late_passed, live = lax.optimization_barrier((late_passed, live))
    late_passed = across(late_passed, 1, owners)
    live, early_passed, *pieces = lax.optimization_barrier([live, early_passed] + pieces)
    near = join_rows(*pieces)
    near, live = lax.optimization_barrier((near, live))
    far = across(near, 1, owners)
    means = gather(False, early, live)
    merged = merge(means, early_passed)
    merged[0], live = lax.optimization_barrier((merged[0], live))
    agg_blocks = dict(zip(early, along(merged, 1, early)))
    means = gather(False, late, live)
    means, *own_blocks = lax.optimization_barrier([means] + own_blocks)
    agg_blocks |= dict(zip(late, along(merge(means, late_passed), 1, late)))
    agg_blocks = [agg_blocks[k] for k in range(pairs)]
    far, near, *agg_blocks = lax.optimization_barrier([far, near] + agg_blocks)
    near_other, far_other = swap(near), swap(far)

    stacked = struct((depth, hops + LANES), BF16)
    own, mean, send = call(
        functools.partial(stack_features, (owners, seeds, fan, fp, seed_rows)),
        "stack_features",
        (stacked, stacked, stacked),
        [VMEM] * (owners + 1),
    )(seed_degree, *own_blocks, *agg_blocks)
    x_other = swap(send)
    logits, hidden, dpre = call(
        functools.partial(forward, (owners, seeds, fan, fp, width, offsets_of(owners))),
        "forward",
        (
            struct((1, seeds, classes), BF16),
            struct((2, seeds, width), BF16),
            struct((hops + LANES, width), BF16),
        ),
        [VMEM] * 10,
        [pltpu.VMEM((depth, width), BF16), pltpu.VMEM((depth, width), BF16)],
        micros=3,
    )(
        seed_degree,
        own,
        mean,
        near,
        far,
        near_other,
        far_other,
        v_self.T,
        v_neigh.T,
        cotangent,
    )
    keep, passed, both = call(
        functools.partial(products, (owners, seeds, fp)),
        "products",
        (
            struct((pairs, fp, width), F32),
            struct((pairs, fp, width), BF16),
            struct((2 * seeds, width), BF16),
        ),
        [VMEM] * 7,
        micros=2,
    )(own, mean, x_other, dpre, swap(dpre), hidden, swap(hidden))
    passed = across(passed, 1, owners)
    hid_near, hid_far = gather_blocks(both, owners)
    blocks = call(
        join_pairs,
        "join_pairs",
        (struct((fp, width), F32),) + (struct((fp, width), BF16),) * (pairs - 1),
        [VMEM] * 2,
    )(keep, passed)
    first, *blocks = along(blocks, -1, range(pairs))
    grad_w, grad_v = call(
        functools.partial(total_gradients, (owners, seeds, f, fp, classes)),
        "total_gradients",
        (struct((f, width), F32), struct((classes, width), F32)),
        [VMEM] * (6 + pairs),
        [pltpu.VMEM((owners * seeds, up(classes, LANES)), BF16)],
    )(first, hid_near, hid_far, near, far, near_other, far_other, *blocks)
    grads = call(
        place_gradients,
        "place_gradients",
        (struct((f, width), F32),) * 2 + (struct((classes, width), F32),) * 2,
        [VMEM] * 4,
    )(grad_w, swap(grad_w), grad_v, swap(grad_v))
    return (logits, grads[0], grads[1], grads[2].T, grads[3].T)


def solution(mesh):
    placed = (
        P(("groups", "rep"), "feat", None),
        P(("groups", "rep"), "feat", None, None),
        P(("groups", "rep"), "feat", None),
        P(("groups", "rep"), None, None, None),
        P(("groups", "rep"), None, None),
        P(("groups", "rep"), None),
        P("feat", None),
        P("feat", None),
        P(),
        P(),
        P(("groups", "rep"), "feat", None),
    )
    return jax.shard_map(
        on_device,
        mesh=mesh,
        in_specs=placed,
        out_specs=(
            P(("groups", "rep"), "feat", None),
            P(("groups", "feat"), None),
            P(("groups", "feat"), None),
            P("groups", None),
            P("groups", None),
        ),
        check_vma=False,
    )
```

```python
import functools

import jax
import jax.numpy as jnp
from jax import lax
from jax.experimental import pallas as pl
from jax.experimental.pallas import tpu as pltpu
from jax.sharding import PartitionSpec as P

F32 = jnp.float32
BF16 = jnp.bfloat16
LANES = 128
PACK = 56
VMEM = pl.BlockSpec(memory_space=pltpu.VMEM)
SMEM = pl.BlockSpec(memory_space=pltpu.SMEM)
HBM = pl.BlockSpec(memory_space=pltpu.HBM)
OVER_FIRST = (((0,), (0,)), ((), ()))
OVER_LAST = (((1,), (1,)), ((), ()))


def up(n, m):
    return -(-n // m) * m


def call(body, name, outs, in_specs, scratch=(), micros=1, vmem=40):
    return pl.pallas_call(
        body,
        name=name,
        out_shape=outs,
        in_specs=in_specs,
        out_specs=jax.tree.map(lambda _: VMEM, outs),
        scratch_shapes=list(scratch),
        compiler_params=pltpu.CompilerParams(vmem_limit_bytes=vmem << 20),
        cost_estimate=pl.CostEstimate(
            flops=0, bytes_accessed=int(micros * 3_000_000), transcendentals=0
        ),
    )


def mix_groups(pieces, seeds, towards):
    groups = LANES // seeds
    shape = next(p for p in pieces if p is not None).shape
    lane_group = lax.broadcasted_iota(jnp.int32, shape, 1) // seeds
    total = jnp.zeros(shape, F32)
    for k, piece in enumerate(pieces):
        if piece is None:
            continue
        turn = (k - towards) % groups
        moved = pltpu.roll(piece, turn * seeds, axis=1) if turn else piece
        total = jnp.where(lane_group == k, moved, total)
    return total


def pack_features(
    sizes,
    idx_ref,
    deg_ref,
    hop_ref,
    seed_ref,
    keep_ref,
    pass_ref,
    live_ref,
    hop,
    packed,
    hop32,
    seed,
    seed32,
    deg,
    idx,
    sems,
):
    owners, seeds, fan, f, fp, nodes = sizes
    groups = LANES // seeds
    hops = fan * seeds
    loads = [
        pltpu.make_async_copy(source, target, sems.at[i])
        for i, (source, target) in enumerate(
            ((idx_ref, idx), (deg_ref, deg), (hop_ref, hop), (seed_ref, seed))
        )
    ]
    for load in loads:
        load.start()
    for load in loads:
        load.wait()
    tiles = owners * seeds // LANES
    for u in range(0, idx.shape[1], 2):
        live = jnp.where(deg[0] > u, idx[0, u], nodes)
        live = live + (jnp.where(deg[0] > u + 1, idx[0, u + 1], nodes) << 16)
        for tile in range(tiles):
            at = (u // 2 * tiles + tile) * fan
            live_ref[at : at + fan, :] = live[:, tile * LANES : (tile + 1) * LANES]
    if fp != f:
        packed[...] = jnp.zeros_like(packed)
        seed32[...] = jnp.zeros_like(seed32)
    for tile in range(owners // groups):
        at = slice(tile * LANES, (tile + 1) * LANES)
        hop32[tile] = hop[0, :, :, at].astype(F32).reshape(f * fan, LANES)
        for block in range(fan // groups):
            taken = [
                hop32[tile, pl.ds(block * groups + k, f, stride=fan), :] for k in range(groups)
            ]
            for e in range(groups):
                packed[tile * groups + e, :f, block * LANES : (block + 1) * LANES] = mix_groups(
                    taken, seeds, e
                ).astype(BF16)
    seed32[:f, :] = seed[0].astype(F32)
    bands = fp // 16
    for tile in range(owners // groups):
        at = slice(tile * LANES, (tile + 1) * LANES)
        for block in range(-(-bands // groups)):
            taken = [
                seed32[(block * groups + k) * 16 : (block * groups + k + 1) * 16, at]
                if block * groups + k < bands
                else None
                for k in range(groups)
            ]
            row, lane = divmod(block * LANES, hops)
            for e in range(groups):
                packed[
                    tile * groups + e, fp + row * 16 : fp + row * 16 + 16, lane : lane + LANES
                ] = mix_groups(taken, seeds, e).astype(BF16)

    side = lax.rem(lax.axis_index("feat"), 2)
    for j in range(owners // 2):
        owner = lax.rem(lax.axis_index("feat") // 2 + j, owners // 2)
        keep_ref[j] = packed[2 * owner + side]
        pass_ref[j] = packed[2 * owner + 1 - side]


def turn_table(f, table, rows):
    nodes = table.shape[2]
    step = 512 if nodes % 512 == 0 else LANES
    lanes = rows.shape[1]
    tail = (lax.broadcasted_iota(jnp.int32, (lanes - f, step), 0) == 0).astype(F32)

    def flip(i, _):
        at = pl.multiple_of(i * step, step)
        block = jnp.concatenate([table[0, :, pl.ds(at, step)].astype(F32), tail], axis=0)
        rows[pl.ds(at, step), :] = block.T
        return 0

    lax.fori_loop(0, nodes // step, flip, 0)
    rows[nodes:, :] = jnp.zeros((8, lanes), F32)


def gather_means(sizes, across_pair, steps, idx, rows, out_ref, picked):
    owners, seeds, fan, f, fp = sizes
    hops = out_ref.shape[2]
    groups = LANES // seeds
    tiles = owners * seeds // LANES
    slots = idx.shape[0] // (tiles * fan * LANES)
    me = lax.axis_index("feat")
    side = lax.rem(me, 2)
    if across_pair:
        side = 1 - side
    for i, step in enumerate(steps):
        owner = 2 * lax.rem(me // 2 + step, owners // 2) + side
        first = owner // groups * (fan * LANES) + lax.rem(owner, groups) * seeds

        def slot_step(t, _):
            src = first + t * LANES
            for k in range(seeds):
                total = None
                for u in range(slots):
                    two = idx[src + (u * tiles * fan * LANES + k)]
                    low = rows[pl.ds(two & 0xFFFF, 1), :]
                    total = low if total is None else total + low
                    total = total + rows[pl.ds(two >> 16, 1), :]
                picked[pl.ds(t * seeds + k, 1), :] = total
            return 0

        lax.fori_loop(0, fan, slot_step, 0)
        flat = picked[...].T
        mean = flat[:f] / flat[f : f + 1]
        if fp != f:
            mean = jnp.concatenate([mean, jnp.zeros((fp - f, hops), F32)], axis=0)
        out_ref[i] = mean.astype(BF16)


def join(first, second, joined):
    joined[: first.shape[0], :] = first[...]
    joined[first.shape[0] :, :] = second[...]


def merge_pairs(keep_ref, pass_ref, *rest):
    count, rows = keep_ref.shape[:2]
    outs = rest
    if len(rest) > count:
        join(rest[0], rest[1], rest[-1])
        outs = rest[2:-1]
    for i, out_ref in enumerate(outs):
        out_ref[:rows, :] = keep_ref[i]
        out_ref[rows:, :] = pass_ref[i]


def my_degrees(seed_degree_ref, seeds):
    half = seed_degree_ref.shape[1]
    wide = jnp.broadcast_to(seed_degree_ref[...], (8, half))
    shift = lax.rem(half - lax.axis_index("feat") * seeds, half)
    mine = pltpu.roll(wide, shift, axis=1)[:, :LANES]
    lane = lax.broadcasted_iota(jnp.int32, (8, LANES), 1)
    return jnp.where(lane < seeds, mine, 1)


def stack_features(sizes, seed_degree_ref, *rest):
    owners, seeds, fan, fp, seed_rows = sizes
    half = owners // 2
    own_blocks, agg_blocks = rest[:half], rest[half:owners]
    own_ref, mean_ref, send_ref = rest[owners:]
    groups = LANES // seeds
    hops = fan * seeds
    own_rows = fp + seed_rows
    lane = lax.broadcasted_iota(jnp.int32, (16, LANES), 1)
    for c in range(owners):
        ref, low = own_blocks[c // 2], c % 2 * own_rows
        own_ref[c * fp : (c + 1) * fp, :hops] = ref[low : low + fp, :]
        mean_ref[c * fp : (c + 1) * fp, :hops] = agg_blocks[c // 2][c % 2 * fp : (c % 2 + 1) * fp, :]
        for band in range(fp // 16):
            row, place = divmod(band * seeds, hops)
            tile = place // LANES
            row = low + fp + row * 16
            block = ref[row : row + 16, tile * LANES : (tile + 1) * LANES].astype(F32)
            turn = (-(band % groups)) % groups
            if turn:
                block = pltpu.roll(block, turn * seeds, axis=1)
            at = c * fp + band * 16
            own_ref[at : at + 16, hops:] = jnp.where(lane < seeds, block, 0.0).astype(BF16)
    degree = my_degrees(seed_degree_ref, seeds)[:1]
    node = lax.broadcasted_iota(jnp.int32, (hops, LANES), 0)
    seed = lax.broadcasted_iota(jnp.int32, (hops, LANES), 1)
    live = (node % seeds == seed) & (node // seeds < degree)
    total = jnp.dot(own_ref[:, :hops], live.astype(F32).astype(BF16), preferred_element_type=F32)
    mean_ref[:, hops:] = (total / degree.astype(F32)).astype(BF16)

    @pl.when(lax.axis_index("rep") == 0)
    def _():
        send_ref[...] = mean_ref[...]

    @pl.when(lax.axis_index("rep") != 0)
    def _():
        send_ref[...] = own_ref[...]


def forward(
    sizes,
    seed_degree_ref,
    own_ref,
    mean_ref,
    near_ref,
    far_ref,
    near_other_ref,
    far_other_ref,
    vs_ref,
    vn_ref,
    cot_ref,
    logits_ref,
    hidden_ref,
    dpre_ref,
    ws,
    wn,
):
    owners, seeds, fan, fp, width, offsets = sizes
    hops = fan * seeds
    half = owners // 2
    me = lax.axis_index("feat")
    block = near_ref.shape[0] // half

    def lay(near, far, w):
        for p, offset in enumerate(offsets):
            source = jnp.bitwise_xor(me, offset)
            c = 2 * lax.rem(me // 2 + half - source // 2, half) + offset % 2
            ref, q = (near, p) if p < half else (far, p - half)
            to = pl.ds(pl.multiple_of(c * fp, fp), fp)
            w[to, :] = ref[q * block : q * block + fp, :]

    @pl.when(lax.axis_index("rep") == 0)
    def _():
        lay(near_ref, far_ref, ws)
        lay(near_other_ref, far_other_ref, wn)

    @pl.when(lax.axis_index("rep") != 0)
    def _():
        lay(near_ref, far_ref, wn)
        lay(near_other_ref, far_other_ref, ws)

    pre = lax.dot_general(own_ref[...], ws[...], OVER_FIRST, preferred_element_type=F32)
    pre = pre + lax.dot_general(mean_ref[...], wn[...], OVER_FIRST, preferred_element_type=F32)
    pre = pre[: hops + seeds]
    sigma = jax.nn.sigmoid(pre)
    hidden = (pre * sigma).astype(BF16)
    slope = sigma * (1.0 + pre * (1.0 - sigma))
    degree = my_degrees(seed_degree_ref, seeds).astype(F32)
    degree = jnp.broadcast_to(degree[:1], (LANES, LANES)).T[:seeds]
    degree = jnp.concatenate([degree] * (width // LANES), axis=1)
    total = jnp.zeros((seeds, width), F32)
    for t in range(fan):
        row = hidden[t * seeds : (t + 1) * seeds].astype(F32)
        total = total + jnp.where(degree > t, row, 0.0)
    hidden_mean = (total / degree).astype(BF16)
    seed_hidden = hidden[hops:]
    hidden_ref[0] = seed_hidden
    hidden_ref[1] = hidden_mean
    logits = lax.dot_general(seed_hidden, vs_ref[...], OVER_LAST, preferred_element_type=F32)
    logits = logits + lax.dot_general(
        hidden_mean, vn_ref[...], OVER_LAST, preferred_element_type=F32
    )
    logits_ref[0] = logits.astype(BF16)
    cot = cot_ref[0]
    back_seed = jnp.dot(cot, vs_ref[...], preferred_element_type=F32)
    back_mean = jnp.dot(cot, vn_ref[...], preferred_element_type=F32)
    back_mean = back_mean / degree
    for t in range(fan):
        at = slice(t * seeds, (t + 1) * seeds)
        dpre_ref[at, :] = (jnp.where(degree > t, back_mean, 0.0) * slope[at]).astype(BF16)
    dpre_ref[hops : hops + seeds, :] = (back_seed * slope[hops:]).astype(BF16)
    dpre_ref[hops + seeds :, :] = jnp.zeros((LANES - seeds, width), BF16)


def products(
    sizes,
    own_ref,
    mean_ref,
    x_ref,
    dpre_ref,
    dpre_other_ref,
    hid_ref,
    hid_other_ref,
    keep_ref,
    pass_ref,
    both_ref,
):
    owners, seeds, fp = sizes

    def run(mine_ref, part):
        total = jnp.dot(mine_ref[...], dpre_ref[...], preferred_element_type=F32)
        total = total + jnp.dot(x_ref[...], dpre_other_ref[...], preferred_element_type=F32)
        for c in range(owners):
            block = total[c * fp : (c + 1) * fp]
            if c % 2:
                pass_ref[c // 2] = block.astype(BF16)
            else:
                keep_ref[c // 2] = block
        both_ref[:seeds, :] = hid_ref[part]
        both_ref[seeds:, :] = hid_other_ref[part]

    @pl.when(lax.axis_index("rep") == 0)
    def _():
        run(own_ref, 0)

    @pl.when(lax.axis_index("rep") != 0)
    def _():
        run(mean_ref, 1)


def join_pairs(keep_ref, passed_ref, first_ref, *outs):
    for i, out_ref in enumerate((first_ref, *outs)):
        total = keep_ref[i] + passed_ref[i].astype(F32)
        out_ref[...] = total.astype(out_ref.dtype)


def total_gradients(sizes, first_ref, hid_near, hid_far, near, far, near_other, far_other, *rest):
    owners, seeds, f, fp, classes = sizes
    half = owners // 2
    blocks = rest[: half - 1]
    grad_w_ref, grad_v_ref, cot = rest[half - 1 :]
    width = first_ref.shape[1]
    split = seeds // 16
    piece = width // split
    block = near.shape[0] // half
    total = first_ref[...]
    for ref in blocks:
        total = total + ref[...].astype(F32)
    grad_w_ref[...] = total[:f]
    grad_v = None
    for hid, mine, other in ((hid_near, near, near_other), (hid_far, far, far_other)):
        for q in range(half):
            for p in range(split):
                at = slice(p * piece, p * piece + cot.shape[1])
                source = slice(q * block + fp, q * block + fp + 16)
                row = q * 2 * seeds + p * 16
                cot[row : row + 16, :] = mine[source, at]
                cot[row + seeds : row + seeds + 16, :] = other[source, at]
        part = lax.dot_general(cot[...], hid[...], OVER_FIRST, preferred_element_type=F32)
        grad_v = part if grad_v is None else grad_v + part
    grad_v_ref[...] = grad_v[:classes]


def place_gradients(w_mine, w_other, v_mine, v_other, ws_ref, wn_ref, vs_ref, vn_ref):
    @pl.when(lax.axis_index("rep") == 0)
    def _():
        ws_ref[...] = w_mine[...]
        wn_ref[...] = w_other[...]
        vs_ref[...] = v_mine[...]
        vn_ref[...] = v_other[...]

    @pl.when(lax.axis_index("rep") != 0)
    def _():
        ws_ref[...] = w_other[...]
        wn_ref[...] = w_mine[...]
        vs_ref[...] = v_other[...]
        vn_ref[...] = v_mine[...]


def swap(x):
    return lax.ppermute(x, "rep", [(0, 1), (1, 0)])


def shift_by(x, step, owners):
    return lax.ppermute(x, "feat", [(k, (k + step) % owners) for k in range(owners)])


def across(x, mask, owners):
    return lax.ppermute(x, "feat", [(k, k ^ mask) for k in range(owners)])


def join_rows(first, second):
    rows, columns = first.shape
    return call(
        join, "join_rows", jax.ShapeDtypeStruct((2 * rows, columns), first.dtype), [VMEM] * 2
    )(first, second)


def gather_blocks(x, owners):
    mask = owners // 2
    while mask > 1:
        x = join_rows(x, across(x, mask, owners))
        mask //= 2
    return x, across(x, 1, owners)


def offsets_of(owners):
    offsets = [0]
    mask = owners // 2
    while mask:
        offsets = offsets + [o ^ mask for o in offsets]
        mask //= 2
    return tuple(offsets)


def on_device(
    seed_feat,
    hop_feat,
    frontier,
    nbr_index,
    hop_degree,
    seed_degree,
    w_self,
    w_neigh,
    v_self,
    v_neigh,
    cotangent,
):
    owners = lax.axis_size("feat")
    seeds, classes = cotangent.shape[1:]
    f, width = w_self.shape
    fan = hop_feat.shape[2]
    nodes = frontier.shape[2]
    hops = fan * seeds
    fp = up(f, 16)
    seed_rows = 16 * -(-(fp // 16) * seeds // hops)
    depth = owners * fp
    struct = jax.ShapeDtypeStruct

    chosen = jnp.where(lax.axis_index("rep") == 0, w_self, w_neigh)
    split = seeds // 16
    pieces = cotangent[0].reshape(split, 16, classes)
    pieces = jnp.pad(pieces, ((0, 0), (0, 0), (0, width // split - classes)))
    message = jnp.concatenate(
        [jnp.pad(chosen, ((0, fp - f), (0, 0)))] + [jnp.concatenate(list(pieces), axis=1)], axis=0
    )
    far_mask = owners // 2
    fetched = across(message, far_mask, owners)
    lanes = up(f + 1, LANES)
    half = owners * seeds
    own_rows = fp + seed_rows
    keep, passed, live = call(
        functools.partial(pack_features, (owners, seeds, fan, f, fp, nodes)),
        "pack_features",
        (
            struct((owners // 2, own_rows, hops), BF16),
            struct((owners // 2, own_rows, hops), BF16),
            struct((nbr_index.size // 2 // LANES, LANES), jnp.int32),
        ),
        [HBM] * 4,
        [
            pltpu.VMEM(hop_feat.shape, BF16),
            pltpu.VMEM((owners, own_rows, hops), BF16),
            pltpu.VMEM((half // LANES, f * fan, LANES), F32),
            pltpu.VMEM(seed_feat.shape, BF16),
            pltpu.VMEM((fp, half), F32),
            pltpu.VMEM(hop_degree.shape, jnp.int32),
            pltpu.VMEM(nbr_index.shape, jnp.int32),
            pltpu.SemaphoreType.DMA((4,)),
        ],
        vmem=PACK,
    )(nbr_index, hop_degree, hop_feat, seed_feat)
    rows = call(
        functools.partial(turn_table, f),
        "turn_table",
        struct((nodes + 8, lanes), F32),
        [VMEM],
    )(frontier)
    live = live.reshape(-1)
    pairs = owners // 2
    passed = across(passed, 1, owners)
    fetched, live, rows = lax.optimization_barrier((fetched, live, rows))
    pieces = [message, fetched]
    mask = far_mask // 2
    while mask > 1:
        joined = join_rows(*pieces)
        joined, live = lax.optimization_barrier((joined, live))
        pieces = [joined, across(joined, mask, owners)]
        mask //= 2

    def gather(across_pair, steps, live):
        return call(
            functools.partial(gather_means, (owners, seeds, fan, f, fp), across_pair, steps),
            "gather_means",
            struct((len(steps), fp, hops), BF16),
            [SMEM, VMEM],
            [pltpu.VMEM((hops, lanes), F32)],
        )(live, rows)

    def merge(keep, passed, pieces=()):
        count, rows = keep.shape[:2]
        outs = (struct((2 * rows, hops), BF16),) * count
        if pieces:
            outs += (struct((2 * pieces[0].shape[0], width), BF16),)
        return list(
            call(merge_pairs, "merge_pairs", outs, [VMEM] * (2 + len(pieces)))(
                keep, passed, *pieces
            )
        )

    def along(blocks, sign, steps):
        return [
            shift_by(x, sign * 2 * k, owners) if k else x for k, x in zip(steps, blocks)
        ]

    order = sorted(range(1, pairs), key=lambda k: (-min(k, pairs - k), k)) + [0]
    early, late = order[: pairs // 2], order[pairs // 2 :]
    early_passed = gather(True, early, live)
    passed, early_passed = lax.optimization_barrier((passed, early_passed))
    merged = merge(keep, passed)
    merged[0], live = lax.optimization_barrier((merged[0], live))
    own_blocks = along(merged, 1, range(pairs))
    early_passed = across(early_passed, 1, owners)
    late_passed = gather(True, late, live)
    late_passed, live = lax.optimization_barrier((late_passed, live))
    late_passed = across(late_passed, 1, owners)
    live, early_passed, *pieces = lax.optimization_barrier([live, early_passed] + pieces)
    near = join_rows(*pieces)
    near, live = lax.optimization_barrier((near, live))
    far = across(near, 1, owners)
    means = gather(False, early, live)
    merged = merge(means, early_passed)
    merged[0], live = lax.optimization_barrier((merged[0], live))
    agg_blocks = dict(zip(early, along(merged, 1, early)))
    means = gather(False, late, live)
    means, *own_blocks = lax.optimization_barrier([means] + own_blocks)
    agg_blocks |= dict(zip(late, along(merge(means, late_passed), 1, late)))
    agg_blocks = [agg_blocks[k] for k in range(pairs)]
    far, near, *agg_blocks = lax.optimization_barrier([far, near] + agg_blocks)
    near_other, far_other = swap(near), swap(far)

    stacked = struct((depth, hops + LANES), BF16)
    own, mean, send = call(
        functools.partial(stack_features, (owners, seeds, fan, fp, seed_rows)),
        "stack_features",
        (stacked, stacked, stacked),
        [VMEM] * (owners + 1),
    )(seed_degree, *own_blocks, *agg_blocks)
    x_other = swap(send)
    logits, hidden, dpre = call(
        functools.partial(forward, (owners, seeds, fan, fp, width, offsets_of(owners))),
        "forward",
        (
            struct((1, seeds, classes), BF16),
            struct((2, seeds, width), BF16),
            struct((hops + LANES, width), BF16),
        ),
        [VMEM] * 10,
        [pltpu.VMEM((depth, width), BF16), pltpu.VMEM((depth, width), BF16)],
        micros=3,
    )(
        seed_degree,
        own,
        mean,
        near,
        far,
        near_other,
        far_other,
        v_self.T,
        v_neigh.T,
        cotangent,
    )
    keep, passed, both = call(
        functools.partial(products, (owners, seeds, fp)),
        "products",
        (
            struct((pairs, fp, width), F32),
            struct((pairs, fp, width), BF16),
            struct((2 * seeds, width), BF16),
        ),
        [VMEM] * 7,
        micros=2,
    )(own, mean, x_other, dpre, swap(dpre), hidden, swap(hidden))
    passed = across(passed, 1, owners)
    hid_near, hid_far = gather_blocks(both, owners)
    blocks = call(
        join_pairs,
        "join_pairs",
        (struct((fp, width), F32),) + (struct((fp, width), BF16),) * (pairs - 1),
        [VMEM] * 2,
    )(keep, passed)
    first, *blocks = along(blocks, -1, range(pairs))
    grad_w, grad_v = call(
        functools.partial(total_gradients, (owners, seeds, f, fp, classes)),
        "total_gradients",
        (struct((f, width), F32), struct((classes, width), F32)),
        [VMEM] * (6 + pairs),
        [pltpu.VMEM((owners * seeds, up(classes, LANES)), BF16)],
    )(first, hid_near, hid_far, near, far, near_other, far_other, *blocks)
    grads = call(
        place_gradients,
        "place_gradients",
        (struct((f, width), F32),) * 2 + (struct((classes, width), F32),) * 2,
        [VMEM] * 4,
    )(grad_w, swap(grad_w), grad_v, swap(grad_v))
    return (logits, grads[0], grads[1], grads[2].T, grads[3].T)


def solution(mesh):
    placed = (
        P(("groups", "rep"), "feat", None),
        P(("groups", "rep"), "feat", None, None),
        P(("groups", "rep"), "feat", None),
        P(("groups", "rep"), None, None, None),
        P(("groups", "rep"), None, None),
        P(("groups", "rep"), None),
        P("feat", None),
        P("feat", None),
        P(),
        P(),
        P(("groups", "rep"), "feat", None),
    )
    return jax.shard_map(
        on_device,
        mesh=mesh,
        in_specs=placed,
        out_specs=(
            P(("groups", "rep"), "feat", None),
            P(("groups", "feat"), None),
            P(("groups", "feat"), None),
            P("groups", None),
            P("groups", None),
        ),
        check_vma=False,
    )
```

```python
import functools

import jax
import jax.numpy as jnp
from jax import lax
from jax.experimental import pallas as pl
from jax.experimental.pallas import tpu as pltpu
from jax.sharding import PartitionSpec as P

F32 = jnp.float32
BF16 = jnp.bfloat16
LANES = 128
PACK = 56
VMEM = pl.BlockSpec(memory_space=pltpu.VMEM)
SMEM = pl.BlockSpec(memory_space=pltpu.SMEM)
HBM = pl.BlockSpec(memory_space=pltpu.HBM)
OVER_FIRST = (((0,), (0,)), ((), ()))
OVER_LAST = (((1,), (1,)), ((), ()))


def up(n, m):
    return -(-n // m) * m


def call(body, name, outs, in_specs, scratch=(), micros=1, vmem=40):
    return pl.pallas_call(
        body,
        name=name,
        out_shape=outs,
        in_specs=in_specs,
        out_specs=jax.tree.map(lambda _: VMEM, outs),
        scratch_shapes=list(scratch),
        compiler_params=pltpu.CompilerParams(vmem_limit_bytes=vmem << 20),
        cost_estimate=pl.CostEstimate(
            flops=0, bytes_accessed=int(micros * 3_000_000), transcendentals=0
        ),
    )


def mix_groups(pieces, seeds, towards):
    groups = LANES // seeds
    shape = next(p for p in pieces if p is not None).shape
    lane_group = lax.broadcasted_iota(jnp.int32, shape, 1) // seeds
    total = jnp.zeros(shape, F32)
    for k, piece in enumerate(pieces):
        if piece is None:
            continue
        turn = (k - towards) % groups
        moved = pltpu.roll(piece, turn * seeds, axis=1) if turn else piece
        total = jnp.where(lane_group == k, moved, total)
    return total


def pack_features(
    sizes,
    idx_ref,
    deg_ref,
    hop_ref,
    seed_ref,
    keep_ref,
    pass_ref,
    live_ref,
    hop,
    packed,
    hop32,
    seed,
    seed32,
    deg,
    idx,
    sems,
):
    owners, seeds, fan, f, fp, nodes = sizes
    groups = LANES // seeds
    hops = fan * seeds
    loads = [
        pltpu.make_async_copy(source, target, sems.at[i])
        for i, (source, target) in enumerate(
            ((idx_ref, idx), (deg_ref, deg), (hop_ref, hop), (seed_ref, seed))
        )
    ]
    for load in loads:
        load.start()
    for load in loads:
        load.wait()
    tiles = owners * seeds // LANES
    for u in range(0, idx.shape[1], 2):
        live = jnp.where(deg[0] > u, idx[0, u], nodes)
        live = live + (jnp.where(deg[0] > u + 1, idx[0, u + 1], nodes) << 16)
        for tile in range(tiles):
            at = (u // 2 * tiles + tile) * fan
            live_ref[at : at + fan, :] = live[:, tile * LANES : (tile + 1) * LANES]
    if fp != f:
        packed[...] = jnp.zeros_like(packed)
        seed32[...] = jnp.zeros_like(seed32)
    for tile in range(owners // groups):
        at = slice(tile * LANES, (tile + 1) * LANES)
        hop32[tile] = hop[0, :, :, at].astype(F32).reshape(f * fan, LANES)
        for block in range(fan // groups):
            taken = [
                hop32[tile, pl.ds(block * groups + k, f, stride=fan), :] for k in range(groups)
            ]
            for e in range(groups):
                packed[tile * groups + e, :f, block * LANES : (block + 1) * LANES] = mix_groups(
                    taken, seeds, e
                ).astype(BF16)
    seed32[:f, :] = seed[0].astype(F32)
    bands = fp // 16
    for tile in range(owners // groups):
        at = slice(tile * LANES, (tile + 1) * LANES)
        for block in range(-(-bands // groups)):
            taken = [
                seed32[(block * groups + k) * 16 : (block * groups + k + 1) * 16, at]
                if block * groups + k < bands
                else None
                for k in range(groups)
            ]
            row, lane = divmod(block * LANES, hops)
            for e in range(groups):
                packed[
                    tile * groups + e, fp + row * 16 : fp + row * 16 + 16, lane : lane + LANES
                ] = mix_groups(taken, seeds, e).astype(BF16)

    side = lax.rem(lax.axis_index("feat"), 2)
    for j in range(owners // 2):
        owner = lax.rem(lax.axis_index("feat") // 2 + j, owners // 2)
        keep_ref[j] = packed[2 * owner + side]
        pass_ref[j] = packed[2 * owner + 1 - side]


def turn_table(f, table, rows):
    nodes = table.shape[2]
    step = 512 if nodes % 512 == 0 else LANES
    lanes = rows.shape[1]
    tail = (lax.broadcasted_iota(jnp.int32, (lanes - f, step), 0) == 0).astype(F32)

    def flip(i, _):
        at = pl.multiple_of(i * step, step)
        block = jnp.concatenate([table[0, :, pl.ds(at, step)].astype(F32), tail], axis=0)
        rows[pl.ds(at, step), :] = block.T
        return 0

    lax.fori_loop(0, nodes // step, flip, 0)
    rows[nodes:, :] = jnp.zeros((8, lanes), F32)


def gather_means(sizes, across_pair, steps, idx, rows, out_ref, picked):
    owners, seeds, fan, f, fp = sizes
    hops = out_ref.shape[2]
    groups = LANES // seeds
    tiles = owners * seeds // LANES
    slots = idx.shape[0] // (tiles * fan * LANES)
    me = lax.axis_index("feat")
    side = lax.rem(me, 2)
    if across_pair:
        side = 1 - side
    for i, step in enumerate(steps):
        owner = 2 * lax.rem(me // 2 + step, owners // 2) + side
        first = owner // groups * (fan * LANES) + lax.rem(owner, groups) * seeds

        def slot_step(t, _):
            src = first + t * LANES
            for k in range(seeds):
                total = None
                for u in range(slots):
                    two = idx[src + (u * tiles * fan * LANES + k)]
                    low = rows[pl.ds(two & 0xFFFF, 1), :]
                    total = low if total is None else total + low
                    total = total + rows[pl.ds(two >> 16, 1), :]
                picked[pl.ds(t * seeds + k, 1), :] = total
            return 0

        lax.fori_loop(0, fan, slot_step, 0)
        flat = picked[...].T
        mean = flat[:f] / flat[f : f + 1]
        if fp != f:
            mean = jnp.concatenate([mean, jnp.zeros((fp - f, hops), F32)], axis=0)
        out_ref[i] = mean.astype(BF16)


def join(first, second, joined):
    joined[: first.shape[0], :] = first[...]
    joined[first.shape[0] :, :] = second[...]


def merge_pairs(keep_ref, pass_ref, *rest):
    count, rows = keep_ref.shape[:2]
    outs = rest
    if len(rest) > count:
        join(rest[0], rest[1], rest[-1])
        outs = rest[2:-1]
    for i, out_ref in enumerate(outs):
        out_ref[:rows, :] = keep_ref[i]
        out_ref[rows:, :] = pass_ref[i]


def my_degrees(seed_degree_ref, seeds):
    half = seed_degree_ref.shape[1]
    wide = jnp.broadcast_to(seed_degree_ref[...], (8, half))
    shift = lax.rem(half - lax.axis_index("feat") * seeds, half)
    mine = pltpu.roll(wide, shift, axis=1)[:, :LANES]
    lane = lax.broadcasted_iota(jnp.int32, (8, LANES), 1)
    return jnp.where(lane < seeds, mine, 1)


def stack_features(sizes, seed_degree_ref, *rest):
    owners, seeds, fan, fp, seed_rows = sizes
    half = owners // 2
    own_blocks, agg_blocks = rest[:half], rest[half:owners]
    own_ref, mean_ref, send_ref = rest[owners:]
    groups = LANES // seeds
    hops = fan * seeds
    own_rows = fp + seed_rows
    lane = lax.broadcasted_iota(jnp.int32, (16, LANES), 1)
    for c in range(owners):
        ref, low = own_blocks[c // 2], c % 2 * own_rows
        own_ref[c * fp : (c + 1) * fp, :hops] = ref[low : low + fp, :]
        mean_ref[c * fp : (c + 1) * fp, :hops] = agg_blocks[c // 2][c % 2 * fp : (c % 2 + 1) * fp, :]
        for band in range(fp // 16):
            row, place = divmod(band * seeds, hops)
            tile = place // LANES
            row = low + fp + row * 16
            block = ref[row : row + 16, tile * LANES : (tile + 1) * LANES].astype(F32)
            turn = (-(band % groups)) % groups
            if turn:
                block = pltpu.roll(block, turn * seeds, axis=1)
            at = c * fp + band * 16
            own_ref[at : at + 16, hops:] = jnp.where(lane < seeds, block, 0.0).astype(BF16)
    degree = my_degrees(seed_degree_ref, seeds)[:1]
    node = lax.broadcasted_iota(jnp.int32, (hops, LANES), 0)
    seed = lax.broadcasted_iota(jnp.int32, (hops, LANES), 1)
    live = (node % seeds == seed) & (node // seeds < degree)
    total = jnp.dot(own_ref[:, :hops], live.astype(F32).astype(BF16), preferred_element_type=F32)
    mean_ref[:, hops:] = (total / degree.astype(F32)).astype(BF16)

    @pl.when(lax.axis_index("rep") == 0)
    def _():
        send_ref[...] = mean_ref[...]

    @pl.when(lax.axis_index("rep") != 0)
    def _():
        send_ref[...] = own_ref[...]


def forward(
    sizes,
    seed_degree_ref,
    own_ref,
    mean_ref,
    near_ref,
    far_ref,
    near_other_ref,
    far_other_ref,
    vs_ref,
    vn_ref,
    cot_ref,
    logits_ref,
    hidden_ref,
    dpre_ref,
    ws,
    wn,
):
    owners, seeds, fan, fp, width, offsets = sizes
    hops = fan * seeds
    half = owners // 2
    me = lax.axis_index("feat")
    block = near_ref.shape[0] // half

    def lay(near, far, w):
        for p, offset in enumerate(offsets):
            source = jnp.bitwise_xor(me, offset)
            c = 2 * lax.rem(me // 2 + half - source // 2, half) + offset % 2
            ref, q = (near, p) if p < half else (far, p - half)
            to = pl.ds(pl.multiple_of(c * fp, fp), fp)
            w[to, :] = ref[q * block : q * block + fp, :]

    @pl.when(lax.axis_index("rep") == 0)
    def _():
        lay(near_ref, far_ref, ws)
        lay(near_other_ref, far_other_ref, wn)

    @pl.when(lax.axis_index("rep") != 0)
    def _():
        lay(near_ref, far_ref, wn)
        lay(near_other_ref, far_other_ref, ws)

    pre = lax.dot_general(own_ref[...], ws[...], OVER_FIRST, preferred_element_type=F32)
    pre = pre + lax.dot_general(mean_ref[...], wn[...], OVER_FIRST, preferred_element_type=F32)
    pre = pre[: hops + seeds]
    sigma = jax.nn.sigmoid(pre)
    hidden = (pre * sigma).astype(BF16)
    slope = sigma * (1.0 + pre * (1.0 - sigma))
    degree = my_degrees(seed_degree_ref, seeds).astype(F32)
    degree = jnp.broadcast_to(degree[:1], (LANES, LANES)).T[:seeds]
    degree = jnp.concatenate([degree] * (width // LANES), axis=1)
    total = jnp.zeros((seeds, width), F32)
    for t in range(fan):
        row = hidden[t * seeds : (t + 1) * seeds].astype(F32)
        total = total + jnp.where(degree > t, row, 0.0)
    hidden_mean = (total / degree).astype(BF16)
    seed_hidden = hidden[hops:]
    hidden_ref[0] = seed_hidden
    hidden_ref[1] = hidden_mean
    logits = lax.dot_general(seed_hidden, vs_ref[...], OVER_LAST, preferred_element_type=F32)
    logits = logits + lax.dot_general(
        hidden_mean, vn_ref[...], OVER_LAST, preferred_element_type=F32
    )
    logits_ref[0] = logits.astype(BF16)
    cot = cot_ref[0]
    back_seed = jnp.dot(cot, vs_ref[...], preferred_element_type=F32)
    back_mean = jnp.dot(cot, vn_ref[...], preferred_element_type=F32)
    back_mean = back_mean / degree
    for t in range(fan):
        at = slice(t * seeds, (t + 1) * seeds)
        dpre_ref[at, :] = (jnp.where(degree > t, back_mean, 0.0) * slope[at]).astype(BF16)
    dpre_ref[hops : hops + seeds, :] = (back_seed * slope[hops:]).astype(BF16)
    dpre_ref[hops + seeds :, :] = jnp.zeros((LANES - seeds, width), BF16)


def products(
    sizes,
    own_ref,
    mean_ref,
    x_ref,
    dpre_ref,
    dpre_other_ref,
    hid_ref,
    hid_other_ref,
    keep_ref,
    pass_ref,
    both_ref,
):
    owners, seeds, fp = sizes

    def run(mine_ref, part):
        total = jnp.dot(mine_ref[...], dpre_ref[...], preferred_element_type=F32)
        total = total + jnp.dot(x_ref[...], dpre_other_ref[...], preferred_element_type=F32)
        for c in range(owners):
            block = total[c * fp : (c + 1) * fp]
            if c % 2:
                pass_ref[c // 2] = block.astype(BF16)
            else:
                keep_ref[c // 2] = block
        both_ref[:seeds, :] = hid_ref[part]
        both_ref[seeds:, :] = hid_other_ref[part]

    @pl.when(lax.axis_index("rep") == 0)
    def _():
        run(own_ref, 0)

    @pl.when(lax.axis_index("rep") != 0)
    def _():
        run(mean_ref, 1)


def join_pairs(keep_ref, passed_ref, first_ref, *outs):
    for i, out_ref in enumerate((first_ref, *outs)):
        total = keep_ref[i] + passed_ref[i].astype(F32)
        out_ref[...] = total.astype(out_ref.dtype)


def total_gradients(sizes, first_ref, hid_near, hid_far, near, far, near_other, far_other, *rest):
    owners, seeds, f, fp, classes = sizes
    half = owners // 2
    blocks = rest[: half - 1]
    grad_w_ref, grad_v_ref, cot = rest[half - 1 :]
    width = first_ref.shape[1]
    split = seeds // 16
    piece = width // split
    block = near.shape[0] // half
    total = first_ref[...]
    for ref in blocks:
        total = total + ref[...].astype(F32)
    grad_w_ref[...] = total[:f]
    grad_v = None
    for hid, mine, other in ((hid_near, near, near_other), (hid_far, far, far_other)):
        for q in range(half):
            for p in range(split):
                at = slice(p * piece, p * piece + cot.shape[1])
                source = slice(q * block + fp, q * block + fp + 16)
                row = q * 2 * seeds + p * 16
                cot[row : row + 16, :] = mine[source, at]
                cot[row + seeds : row + seeds + 16, :] = other[source, at]
        part = lax.dot_general(cot[...], hid[...], OVER_FIRST, preferred_element_type=F32)
        grad_v = part if grad_v is None else grad_v + part
    grad_v_ref[...] = grad_v[:classes]


def place_gradients(w_mine, w_other, v_mine, v_other, ws_ref, wn_ref, vs_ref, vn_ref):
    @pl.when(lax.axis_index("rep") == 0)
    def _():
        ws_ref[...] = w_mine[...]
        wn_ref[...] = w_other[...]
        vs_ref[...] = v_mine[...]
        vn_ref[...] = v_other[...]

    @pl.when(lax.axis_index("rep") != 0)
    def _():
        ws_ref[...] = w_other[...]
        wn_ref[...] = w_mine[...]
        vs_ref[...] = v_other[...]
        vn_ref[...] = v_mine[...]


def swap(x):
    return lax.ppermute(x, "rep", [(0, 1), (1, 0)])


def shift_by(x, step, owners):
    return lax.ppermute(x, "feat", [(k, (k + step) % owners) for k in range(owners)])


def across(x, mask, owners):
    return lax.ppermute(x, "feat", [(k, k ^ mask) for k in range(owners)])


def join_rows(first, second):
    rows, columns = first.shape
    return call(
        join, "join_rows", jax.ShapeDtypeStruct((2 * rows, columns), first.dtype), [VMEM] * 2
    )(first, second)


def gather_blocks(x, owners):
    mask = owners // 2
    while mask > 1:
        x = join_rows(x, across(x, mask, owners))
        mask //= 2
    return x, across(x, 1, owners)


def offsets_of(owners):
    offsets = [0]
    mask = owners // 2
    while mask:
        offsets = offsets + [o ^ mask for o in offsets]
        mask //= 2
    return tuple(offsets)


def on_device(
    seed_feat,
    hop_feat,
    frontier,
    nbr_index,
    hop_degree,
    seed_degree,
    w_self,
    w_neigh,
    v_self,
    v_neigh,
    cotangent,
):
    owners = lax.axis_size("feat")
    seeds, classes = cotangent.shape[1:]
    f, width = w_self.shape
    fan = hop_feat.shape[2]
    nodes = frontier.shape[2]
    hops = fan * seeds
    fp = up(f, 16)
    seed_rows = 16 * -(-(fp // 16) * seeds // hops)
    depth = owners * fp
    struct = jax.ShapeDtypeStruct

    chosen = jnp.where(lax.axis_index("rep") == 0, w_self, w_neigh)
    split = seeds // 16
    pieces = cotangent[0].reshape(split, 16, classes)
    pieces = jnp.pad(pieces, ((0, 0), (0, 0), (0, width // split - classes)))
    message = jnp.concatenate(
        [jnp.pad(chosen, ((0, fp - f), (0, 0)))] + [jnp.concatenate(list(pieces), axis=1)], axis=0
    )
    far_mask = owners // 2
    fetched = across(message, far_mask, owners)
    lanes = up(f + 1, LANES)
    half = owners * seeds
    own_rows = fp + seed_rows
    keep, passed, live = call(
        functools.partial(pack_features, (owners, seeds, fan, f, fp, nodes)),
        "pack_features",
        (
            struct((owners // 2, own_rows, hops), BF16),
            struct((owners // 2, own_rows, hops), BF16),
            struct((nbr_index.size // 2 // LANES, LANES), jnp.int32),
        ),
        [HBM] * 4,
        [
            pltpu.VMEM(hop_feat.shape, BF16),
            pltpu.VMEM((owners, own_rows, hops), BF16),
            pltpu.VMEM((half // LANES, f * fan, LANES), F32),
            pltpu.VMEM(seed_feat.shape, BF16),
            pltpu.VMEM((fp, half), F32),
            pltpu.VMEM(hop_degree.shape, jnp.int32),
            pltpu.VMEM(nbr_index.shape, jnp.int32),
            pltpu.SemaphoreType.DMA((4,)),
        ],
        vmem=PACK,
    )(nbr_index, hop_degree, hop_feat, seed_feat)
    rows = call(
        functools.partial(turn_table, f),
        "turn_table",
        struct((nodes + 8, lanes), F32),
        [VMEM],
    )(frontier)
    live = live.reshape(-1)
    pairs = owners // 2
    passed = across(passed, 1, owners)
    fetched, live, rows = lax.optimization_barrier((fetched, live, rows))
    pieces = [message, fetched]
    mask = far_mask // 2
    while mask > 1:
        joined = join_rows(*pieces)
        joined, live = lax.optimization_barrier((joined, live))
        pieces = [joined, across(joined, mask, owners)]
        mask //= 2

    def gather(across_pair, steps, live):
        return call(
            functools.partial(gather_means, (owners, seeds, fan, f, fp), across_pair, steps),
            "gather_means",
            struct((len(steps), fp, hops), BF16),
            [SMEM, VMEM],
            [pltpu.VMEM((hops, lanes), F32)],
        )(live, rows)

    def merge(keep, passed, pieces=()):
        count, rows = keep.shape[:2]
        outs = (struct((2 * rows, hops), BF16),) * count
        if pieces:
            outs += (struct((2 * pieces[0].shape[0], width), BF16),)
        return list(
            call(merge_pairs, "merge_pairs", outs, [VMEM] * (2 + len(pieces)))(
                keep, passed, *pieces
            )
        )

    def along(blocks, sign, steps):
        return [
            shift_by(x, sign * 2 * k, owners) if k else x for k, x in zip(steps, blocks)
        ]

    order = sorted(range(1, pairs), key=lambda k: (-min(k, pairs - k), -k)) + [0]
    early, late = order[: pairs // 2], order[pairs // 2 :]
    early_passed = gather(True, early, live)
    passed, early_passed = lax.optimization_barrier((passed, early_passed))
    merged = merge(keep, passed)
    merged[0], live = lax.optimization_barrier((merged[0], live))
    own_blocks = along(merged, 1, range(pairs))
    early_passed = across(early_passed, 1, owners)
    late_passed = gather(True, late, live)
    late_passed, live = lax.optimization_barrier((late_passed, live))
    late_passed = across(late_passed, 1, owners)
    live, early_passed, *pieces = lax.optimization_barrier([live, early_passed] + pieces)
    near = join_rows(*pieces)
    near, live = lax.optimization_barrier((near, live))
    far = across(near, 1, owners)
    means = gather(False, early, live)
    merged = merge(means, early_passed)
    merged[0], live = lax.optimization_barrier((merged[0], live))
    agg_blocks = dict(zip(early, along(merged, 1, early)))
    means = gather(False, late, live)
    means, *own_blocks = lax.optimization_barrier([means] + own_blocks)
    agg_blocks |= dict(zip(late, along(merge(means, late_passed), 1, late)))
    agg_blocks = [agg_blocks[k] for k in range(pairs)]
    far, near, *agg_blocks = lax.optimization_barrier([far, near] + agg_blocks)
    near_other, far_other = swap(near), swap(far)

    stacked = struct((depth, hops + LANES), BF16)
    own, mean, send = call(
        functools.partial(stack_features, (owners, seeds, fan, fp, seed_rows)),
        "stack_features",
        (stacked, stacked, stacked),
        [VMEM] * (owners + 1),
    )(seed_degree, *own_blocks, *agg_blocks)
    x_other = swap(send)
    logits, hidden, dpre = call(
        functools.partial(forward, (owners, seeds, fan, fp, width, offsets_of(owners))),
        "forward",
        (
            struct((1, seeds, classes), BF16),
            struct((2, seeds, width), BF16),
            struct((hops + LANES, width), BF16),
        ),
        [VMEM] * 10,
        [pltpu.VMEM((depth, width), BF16), pltpu.VMEM((depth, width), BF16)],
        micros=3,
    )(
        seed_degree,
        own,
        mean,
        near,
        far,
        near_other,
        far_other,
        v_self.T,
        v_neigh.T,
        cotangent,
    )
    keep, passed, both = call(
        functools.partial(products, (owners, seeds, fp)),
        "products",
        (
            struct((pairs, fp, width), F32),
            struct((pairs, fp, width), BF16),
            struct((2 * seeds, width), BF16),
        ),
        [VMEM] * 7,
        micros=2,
    )(own, mean, x_other, dpre, swap(dpre), hidden, swap(hidden))
    passed = across(passed, 1, owners)
    hid_near, hid_far = gather_blocks(both, owners)
    blocks = call(
        join_pairs,
        "join_pairs",
        (struct((fp, width), F32),) + (struct((fp, width), BF16),) * (pairs - 1),
        [VMEM] * 2,
    )(keep, passed)
    first, *blocks = along(blocks, -1, range(pairs))
    grad_w, grad_v = call(
        functools.partial(total_gradients, (owners, seeds, f, fp, classes)),
        "total_gradients",
        (struct((f, width), F32), struct((classes, width), F32)),
        [VMEM] * (6 + pairs),
        [pltpu.VMEM((owners * seeds, up(classes, LANES)), BF16)],
    )(first, hid_near, hid_far, near, far, near_other, far_other, *blocks)
    grads = call(
        place_gradients,
        "place_gradients",
        (struct((f, width), F32),) * 2 + (struct((classes, width), F32),) * 2,
        [VMEM] * 4,
    )(grad_w, swap(grad_w), grad_v, swap(grad_v))
    return (logits, grads[0], grads[1], grads[2].T, grads[3].T)


def solution(mesh):
    placed = (
        P(("groups", "rep"), "feat", None),
        P(("groups", "rep"), "feat", None, None),
        P(("groups", "rep"), "feat", None),
        P(("groups", "rep"), None, None, None),
        P(("groups", "rep"), None, None),
        P(("groups", "rep"), None),
        P("feat", None),
        P("feat", None),
        P(),
        P(),
        P(("groups", "rep"), "feat", None),
    )
    return jax.shard_map(
        on_device,
        mesh=mesh,
        in_specs=placed,
        out_specs=(
            P(("groups", "rep"), "feat", None),
            P(("groups", "feat"), None),
            P(("groups", "feat"), None),
            P("groups", None),
            P("groups", None),
        ),
        check_vma=False,
    )
```
